256 devices in a mesh: ctx: 8 (over x, z_hi), serve: 32 (over z_lo, y, core).
Axes of the slice: x: 4, y: 4, z: 8 (z_hi: 2, z_lo: 4; z = z_hi * 4 + z_lo), core: 2. Of those that a mesh axis runs over, the one named last changes fastest.
Arguments:
- queries: bfloat16 [8192, 8192], P(('ctx', 'serve')), may hold values from -6 to 6
- key_rows: bfloat16 [8192, 1024], P(('ctx', 'serve')), may hold values from -6 to 6
- value_rows: bfloat16 [8192, 1024], P(('ctx', 'serve')), may hold values from -6 to 6
- page_owner: int32 [512], P('ctx'), may hold values from 0 to 31, as said below
- page_slot: int32 [512], P('ctx'), may hold values from 0 to 3, as said below
Outputs:
- attended: bfloat16 [8192, 8192], P(('ctx', 'serve'))
- key_cache: bfloat16 [1024, 16, 1024], P(('ctx', 'serve'))
- value_cache: bfloat16 [1024, 16, 1024], P(('ctx', 'serve'))
The draws below stay inside these ranges and needn't reach their ends.
Inputs may be any that keep to these rules, and one draw needn't show every extreme that they name: `page_owner`: within each block of 64 consecutive pages some owner receives exactly 4 pages and no owner more. `page_slot`: within each block of 64 consecutive pages no owner receives two pages in one slot.
All inputs are finite; a program needn't handle non-finite values.
Results may differ from the reference program's by a relative error of at most 0.0065.
Values may be sent and summed in bfloat16 or wider, within the bound.
A program may use at most 64 MiB of HBM per device.

```python
import math
import jax
import jax.numpy as jnp
from jax import lax

HEADS = 64
KV_HEADS = 8
HEAD_DIM = 128
TOK_DEV = 1024
PAGE = 16
TOKENS = 8192
PAGES = 512
SLOTS = 4
N_CTX = 8
N_SERVE = 32


def base_entries(key, width):
    return jnp.clip(jax.random.normal(key, (TOKENS, width), jnp.float32), -6.0, 6.0)


def draw_queries(key, part):
    key = jax.random.fold_in(key, 3)
    entries = base_entries(key, HEADS * HEAD_DIM).reshape(TOKENS, HEADS, HEAD_DIM)
    return entries.reshape(TOKENS, HEADS * HEAD_DIM).astype(jnp.bfloat16)


def draw_key_rows(key, part):
    key = jax.random.fold_in(key, 5)
    entries = base_entries(key, KV_HEADS * HEAD_DIM).reshape(TOKENS, KV_HEADS, HEAD_DIM)
    return entries.reshape(TOKENS, KV_HEADS * HEAD_DIM).astype(jnp.bfloat16)


def placement_lists(key):
    per_block = TOK_DEV // PAGE
    block_count = PAGES // per_block
    owner_count = 2 * per_block // SLOTS
    entry_index = jnp.arange(per_block, dtype=jnp.int32)
    owner_rank = jnp.where(entry_index < SLOTS, 0, 1 + (entry_index - SLOTS) % (owner_count - 1))
    within = jnp.where(entry_index < SLOTS, entry_index, (entry_index - SLOTS) // (owner_count - 1))

    def one_block(block_key):
        order_key, owner_key, offset_key = jax.random.split(block_key, 3)
        page_order = jax.random.permutation(order_key, per_block)
        owner_table = jax.random.permutation(owner_key, owner_count)
        offsets = jax.random.randint(offset_key, (owner_count,), 0, SLOTS)
        owner_at = owner_table[owner_rank]
        slot_at = (within + offsets[owner_at]) % SLOTS
        owners = jnp.zeros((per_block,), jnp.int32).at[page_order].set(owner_at.astype(jnp.int32))
        slots_of = jnp.zeros((per_block,), jnp.int32).at[page_order].set(slot_at.astype(jnp.int32))
        return (owners, slots_of)
    block_keys = jax.random.split(key, block_count)
    owners, slots_of = jax.vmap(one_block)(block_keys)
    return (owners.reshape(-1), slots_of.reshape(-1))


def draw_page_owner(key, part):
    owners, slots_of = placement_lists(key)
    return owners


def draw_page_slot(key, part):
    owners, slots_of = placement_lists(key)
    return slots_of


def levels(own_key, shape, cuts, least, top_value):
    gain, own = 1.0, jax.random.fold_in(own_key, 6)
    for position, blocks in cuts:
        heights = jnp.exp(jax.random.uniform(jax.random.fold_in(own, position), (blocks,), jnp.float32, least / len(cuts), top_value / len(cuts)))
        gain = gain * jnp.repeat(heights, shape[position] // blocks).reshape([-1 if axis == position else 1 for axis in range(len(shape))])
    return gain


def gaussian(key, dims, deviation, reach, shards=(), kind=jnp.bfloat16):
    array = jax.random.normal(key, dims, jnp.float32) * deviation
    if len(shards) > 0:
        array = levels(key, dims, shards, -0.22, 0.18) * array
    return jnp.clip(array, min=-reach, max=reach).astype(kind)


def setup_inputs(seed: int = 0) -> dict:
    keys = jax.random.split(jax.random.key(seed), 6)
    return {
        "queries": draw_queries(jax.random.fold_in(keys[5], 71), 0),
        "key_rows": draw_key_rows(jax.random.fold_in(keys[5], 71), 0),
        "value_rows": gaussian(keys[2], (TOKENS, KV_HEADS * HEAD_DIM), 1.0, 6.0, ((0, 256),)),
        "page_owner": draw_page_owner(jax.random.fold_in(keys[5], 71), 0),
        "page_slot": draw_page_slot(jax.random.fold_in(keys[5], 71), 0),
    }


def reference(queries, key_rows, value_rows, page_owner, page_slot):
    group_size = HEADS // KV_HEADS
    query_heads = queries.reshape(TOKENS, HEADS, HEAD_DIM).transpose(1, 0, 2)
    key_heads = key_rows.reshape(TOKENS, KV_HEADS, HEAD_DIM).transpose(1, 0, 2)
    value_heads = value_rows.reshape(TOKENS, KV_HEADS, HEAD_DIM).transpose(1, 0, 2)
    token_pos = jnp.arange(TOKENS, dtype=jnp.int32)
    causal = token_pos[None, :] <= token_pos[:, None]
    score_scale = 1.0 / math.sqrt(HEAD_DIM)

    def one_head(head_args):
        query_head, head_index = head_args
        key_head = key_heads[head_index // group_size]
        value_head = value_heads[head_index // group_size]
        scores = jnp.dot(query_head, key_head.T, preferred_element_type=jnp.float32) * score_scale
        scores = jnp.where(causal, scores, -1e+30)
        row_max = lax.optimization_barrier(jnp.max(scores, axis=-1, keepdims=True))
        expo = jnp.where(causal, jnp.exp(scores - row_max), 0.0)
        row_total = lax.optimization_barrier(jnp.sum(expo, axis=-1, keepdims=True))
        weights = expo.astype(jnp.bfloat16)
        summed = jnp.dot(weights, value_head, preferred_element_type=jnp.float32)
        return (summed / row_total).astype(jnp.bfloat16)
    result = lax.map(one_head, (query_heads, jnp.arange(HEADS, dtype=jnp.int32)))
    attended = result.transpose(1, 0, 2).reshape(TOKENS, HEADS * HEAD_DIM)
    per_block = TOK_DEV // PAGE
    page_ids = jnp.arange(PAGES, dtype=jnp.int32)
    target_rows = (page_ids // per_block * N_SERVE + page_owner) * SLOTS + page_slot
    kv_width = KV_HEADS * HEAD_DIM
    empty_cache = jnp.zeros((N_CTX * N_SERVE * SLOTS, PAGE, kv_width), jnp.bfloat16)
    key_cache = empty_cache.at[target_rows].set(key_rows.reshape(PAGES, PAGE, kv_width))
    value_cache = empty_cache.at[target_rows].set(value_rows.reshape(PAGES, PAGE, kv_width))
    return (attended, key_cache, value_cache)
```

```python
import functools
import math

import jax
import jax.numpy as jnp
from jax import lax
from jax.experimental import pallas as pl
from jax.experimental.pallas import tpu as pltpu
from jax.sharding import PartitionSpec as P

HEAD_DIM = 128
ROWS = 32
GROUP = 8
HALF = 512
SET = 1024
SCALE = math.log2(math.e) / math.sqrt(HEAD_DIM)
LOW = -1e30
NT = (((1,), (1,)), ((), ()))
MESH = pl.DeviceIdType.MESH


def device(x, zz, p, y, c):
    return (x * 2 + zz // 2, ((zz % 2) * 2 + p) * 8 + y * 2 + c)


def kernel(
    q_in, k_in, v_in, owner, slot,
    att, key_cache, value_cache,
    q_land, v_land, kv, acc, top, o_stage, pages,
    kv_send, kv_recv, q_send, q_recv, z_send, z_recv, x_send, x_recv,
    s_send, s_recv, o_send, o_recv, g_send, g_recv,
):
    ctx = lax.axis_index("ctx")
    serve = lax.axis_index("serve")
    x = ctx // 2
    zz = (ctx % 2) * 2 + serve // 16
    p = (serve // 8) % 2
    y = (serve // 2) % 4
    c = serve % 2
    mine = p * 4 + y
    head = y * 2 + p
    x_up, x_down = (x + 1) % 4, (x + 3) % 4
    z_up, z_down = (zz + 1) % 4, (zz + 3) % 4

    def at_x(other):
        return device(other, zz, p, y, c)

    def at_z(other):
        return device(x, other, p, y, c)

    sibling = device(x, zz, p, y, 1 - c)

    def partner(i):
        k = (mine + i) % GROUP
        return k, k // 4, k % 4

    barrier = pltpu.get_barrier_semaphore()
    peers = [sibling, at_x(x_up), at_x(x_down), at_z(z_up), at_z(z_down)]
    for i in range(1, GROUP):
        k, pd, yd = partner(i)
        peers.append(device(x, zz, pd, yd, c))
        peers.append(device(3 - x, zz, pd, yd, c))
    for peer in peers:
        pl.semaphore_signal(barrier, inc=1, device_id=peer, device_id_type=MESH)
    pl.semaphore_wait(barrier, len(peers))

    def cols(start, size):
        return pl.ds(pl.multiple_of(start, 128), size)

    def rows(start):
        return pl.ds(pl.multiple_of(start, ROWS), ROWS)

    def k_copy(i):
        k, pd, yd = partner(i)
        return dict(
            src_ref=k_in.at[:, cols((yd * 2 + pd) * 128, 128)],
            dst_ref=kv.at[0, 0, c, rows(mine * ROWS), :],
        ), device(x, zz, pd, yd, c)

    def v_copy(i):
        k, pd, yd = partner(i)
        return dict(
            src_ref=v_in.at[:, cols((yd * 2 + pd) * 128, 128)],
            dst_ref=v_land.at[mine],
        ), device(x, zz, pd, yd, c)

    def q_copy(i, which):
        k, pd, yd = partner(i)
        return dict(
            src_ref=q_in.at[:, cols((yd * 2 + pd) * 1024 + which * HALF, HALF)],
            dst_ref=q_land.at[which, mine],
        ), device(x if which == 0 else 3 - x, zz, pd, yd, c)

    def remote(refs, to, send, recv):
        return pltpu.make_async_remote_copy(
            **refs, send_sem=send, recv_sem=recv, device_id=to, device_id_type=MESH
        )

    def local(refs, sem):
        return pltpu.make_async_copy(refs["src_ref"], refs["dst_ref"], sem)

    sends = []
    for i in range(1, GROUP):
        for which, make in ((0, k_copy), (1, v_copy)):
            refs, to = make(i)
            sends.append(remote(refs, to, kv_send.at[which, i], kv_recv.at[which]))
    for which, make in ((0, k_copy), (1, v_copy)):
        local(make(0)[0], kv_recv.at[which]).start()
    for copy in sends:
        copy.start()
    for which in range(2):
        for i in range(GROUP):
            refs, to = q_copy(i, which)
            if which == 0 and i == 0:
                local(refs, q_recv.at[0]).start()
            else:
                copy = remote(refs, to, q_send.at[which, i], q_recv.at[which])
                copy.start()
                sends.append(copy)

    acc[...] = jnp.zeros_like(acc)
    top[...] = jnp.full_like(top, LOW)

    def arrived(ref, sem):
        pltpu.make_async_copy(ref, ref, sem).wait()

    def whole(dx, dz):
        return kv.at[dx, dz, c]

    def part(dx, dz, which):
        return kv.at[dx, dz, c, pl.ds(which * 256, 256), :]

    def ring(src, dst, to, send, recv):
        return remote(dict(src_ref=src, dst_ref=dst), to, send, recv)

    def to_sibling(dx, dz):
        n = dx * 4 + dz
        return ring(whole(dx, dz), whole(dx, dz), sibling, s_send.at[n], s_recv.at[n])

    z_copies = [
        ring(whole(0, 0), whole(0, 3), at_z(z_up), z_send.at[0], z_recv.at[0]),
        ring(whole(0, 0), whole(0, 1), at_z(z_down), z_send.at[1], z_recv.at[1]),
        ring(part(0, 3, 0), part(0, 2, 0), at_z(z_up), z_send.at[2], z_recv.at[2]),
        ring(part(0, 1, 1), part(0, 2, 1), at_z(z_down), z_send.at[3], z_recv.at[3]),
    ]

    def x_near(dz, way):
        if way == 0:
            return ring(whole(0, dz), whole(3, dz), at_x(x_up), x_send.at[0, dz], x_recv.at[0, dz])
        return ring(whole(0, dz), whole(1, dz), at_x(x_down), x_send.at[1, dz], x_recv.at[1, dz])

    def x_far(dz, way):
        if way == 0:
            return ring(part(3, dz, 0), part(2, dz, 0), at_x(x_up), x_send.at[2, dz], x_recv.at[2, dz])
        return ring(part(1, dz, 1), part(2, dz, 1), at_x(x_down), x_send.at[3, dz], x_recv.at[3, dz])

    def spread(dz):
        x_near(dz, 0).start()
        x_near(dz, 1).start()
        to_sibling(0, dz).start()

    arrived(kv.at[0, 0, c, pl.ds(0, 256), :], kv_recv.at[0])
    arrived(v_land, kv_recv.at[1])
    v_turned = v_land[...].reshape(256, HEAD_DIM).T
    kv[0, 0, c, 256:384, :] = v_turned[:, 0:128]
    kv[0, 0, c, 384:512, :] = v_turned[:, 128:256]
    z_copies[0].start()
    z_copies[1].start()
    spread(0)
    z_copies[0].wait_recv()
    z_copies[2].start()
    spread(3)
    z_copies[1].wait_recv()
    z_copies[3].start()
    spread(1)
    z_copies[2].wait_recv()
    z_copies[3].wait_recv()
    spread(2)
    arrived(q_land.at[0], q_recv.at[0])
    arrived(q_land.at[1], q_recv.at[1])
    for dz in range(4):
        to_sibling(0, dz).wait_recv()

    def operands(which, dx):
        q = q_land[which]
        q = jnp.concatenate(
            [q[:, :, h * 128 : (h + 1) * 128].reshape(256, HEAD_DIM) for h in range(4)], axis=0
        )
        key = jnp.concatenate(
            [kv[dx, dz, core, 0:256, :] for dz in range(4) for core in range(2)], axis=0
        )
        value = jnp.concatenate(
            [
                kv[dx, dz, core, at : at + 128, :]
                for dz in range(4)
                for core in range(2)
                for at in (256, 384)
            ],
            axis=1,
        )
        value = jnp.concatenate([value, jnp.ones((16, 2048), jnp.bfloat16)], axis=0)
        scores = lax.dot_general(key, q, NT, preferred_element_type=jnp.float32) * SCALE
        return scores, value

    def finish(which, old, new, weights, value):
        product = jnp.dot(value, weights, preferred_element_type=jnp.float32)
        acc[which] = acc[which] * jnp.exp2(old - new)[0:1] + product
        top[which] = new

    def visit_all(which, dx):
        scores, value = operands(which, dx)
        old = top[which]
        new = jnp.maximum(old, jnp.max(scores, axis=0, keepdims=True))
        weights = jnp.exp2(scores - new[0:1]).astype(jnp.bfloat16)
        finish(which, old, new, weights, value)

    def visit_causal(which, dx):
        scores, value = operands(which, dx)
        key_row = lax.broadcasted_iota(jnp.int32, (512, 1), 0)
        key_pos = (key_row % 256 // 32) * 64 + (key_row // 256) * 32 + key_row % 32
        query_row = lax.broadcasted_iota(jnp.int32, (1, SET), 1) % 256
        query_pos = (query_row // 32) * 64 + c * 32 + query_row % 32
        old = top[which]
        pieces = [jnp.where(key_pos <= query_pos, scores[0:512], LOW)]
        new = jnp.maximum(old, jnp.max(pieces[0], axis=0, keepdims=True))
        for dz in range(1, 4):
            pieces.append(scores[dz * 512 : (dz + 1) * 512])
            high = jnp.max(pieces[dz], axis=0, keepdims=True)
            new = jnp.where(zz + dz >= 4, jnp.maximum(new, high), new)
        weights = []
        for dz in range(4):
            base = new[0:1] if dz == 0 else jnp.where(zz + dz >= 4, new[0:1], -LOW)
            weights.append(jnp.exp2(pieces[dz] - base).astype(jnp.bfloat16))
        finish(which, old, new, jnp.concatenate(weights, axis=0), value)

    def place_pages():
        row = lax.broadcasted_iota(jnp.int32, (512, 1), 0)
        k = row // 64
        target = ((zz % 2) * 2 + k // 4) * 32 + (k % 4) * 8 + c * 4 + (row // 16) % 4
        row_key = target * 16 + row % 16
        lane = lax.broadcasted_iota(jnp.int32, (1, 256), 1)
        found_k = jnp.zeros((512, HEAD_DIM), jnp.float32)
        found_v = jnp.zeros((512, HEAD_DIM), jnp.float32)
        for other in range(2):
            low = (zz + other) % 2
            dz = 0 if other == 0 else 1 + 2 * (zz % 2)
            for core in range(2):
                token = jnp.zeros((1, 256), jnp.int32)
                for i in range(16):
                    page = low * 32 + (i // 2) * 4 + core * 2 + i % 2
                    code = owner[page] * 4 + slot[page]
                    token = jnp.where(lane // 16 == i, code, token)
                token = token * 16 + lane % 16
                pick = jnp.where(row_key == token, 1.0, 0.0).astype(jnp.bfloat16)
                found_k += jnp.dot(
                    pick, kv[0, dz, core, 0:256, :],
                    preferred_element_type=jnp.float32,
                )
                turned = jnp.concatenate(
                    [kv[0, dz, core, 256:384, :], kv[0, dz, core, 384:512, :]], axis=1
                )
                found_v += lax.dot_general(pick, turned, NT, preferred_element_type=jnp.float32)
        pages[0] = found_k.astype(jnp.bfloat16).reshape(32, 16, HEAD_DIM)
        pages[1] = found_v.astype(jnp.bfloat16).reshape(32, 16, HEAD_DIM)

    def page_copy(i, which):
        k, pd, yd = partner(i)
        cache = (key_cache, value_cache)[which]
        return dict(
            src_ref=pages.at[which, pl.ds(k * 4, 4)],
            dst_ref=cache.at[:, :, cols(head * 128, 128)],
        ), device(x, zz, pd, yd, c)

    def send_pages():
        for which in range(2):
            local(page_copy(0, which)[0], g_recv.at[which]).start()
            for i in range(1, GROUP):
                refs, to = page_copy(i, which)
                remote(refs, to, g_send.at[which, i], g_recv.at[which]).start()

    def near():
        for dz in (0, 3, 1, 2):
            x_near(dz, 0).wait_recv()
            x_far(dz, 0).start()
            to_sibling(3, dz).start()
            x_near(dz, 1).wait_recv()
            x_far(dz, 1).start()
            to_sibling(1, dz).start()
        for dz in range(4):
            to_sibling(3, dz).wait_recv()
            to_sibling(1, dz).wait_recv()

    def far():
        for dz in (0, 3, 1, 2):
            x_far(dz, 0).wait_recv()
            x_far(dz, 1).wait_recv()
            to_sibling(2, dz).start()
        for dz in range(4):
            to_sibling(2, dz).wait_recv()

    def by_x(t, table):
        value = jnp.int32(0)
        for xi, entries in enumerate(table):
            for ti, entry in enumerate(entries):
                if entry:
                    value = value + jnp.where((x == xi) & (t == ti), entry, 0)
        return value

    sets = ((0, 1, 1, 1, 1), (0, 1, 0, 1, 1), (0, 0, 1, 0, 1), (0, 0, 1, 0, 0))
    steps = ((0, 0, 1, 3, 2), (0, 0, 3, 3, 1), (0, 3, 3, 2, 2), (0, 1, 1, 3, 2))
    causal = ((1, 0, 0, 1, 0), (1, 0, 0, 0, 1), (1, 0, 1, 0, 0), (1, 0, 1, 0, 0))

    def step(t, carry):
        @pl.when(t == 1)
        def _():
            place_pages()
            send_pages()

        @pl.when(t == jnp.where(x >= 2, 1, 2))
        def _():
            near()

        @pl.when(t == 3)
        def _():
            far()

        which = by_x(t, sets)
        dx = by_x(t, steps)
        own = by_x(t, causal)

        @pl.when(own == 1)
        def _():
            visit_causal(which, dx)

        @pl.when(own == 0)
        def _():
            visit_all(which, dx)

        return carry

    lax.fori_loop(0, 5, step, 0)

    def o_copy(i, which):
        k, pd, yd = partner(i)
        return dict(
            src_ref=o_stage.at[which, k],
            dst_ref=att.at[:, cols(head * 1024 + which * HALF, HALF)],
        ), device(x if which == 0 else 3 - x, zz, pd, yd, c)

    for which in range(2):
        total = acc[which, 128:129, :]
        done = acc[which, 0:128, :] / total
        for h in range(4):
            o_stage[which, :, :, h * 128 : (h + 1) * 128] = (
                done[:, h * 256 : (h + 1) * 256].T.astype(jnp.bfloat16).reshape(GROUP, ROWS, HEAD_DIM)
            )
        for i in range(GROUP):
            refs, to = o_copy(i, which)
            if which == 0 and i == 0:
                local(refs, o_recv).start()
            else:
                copy = remote(refs, to, o_send.at[which, i], o_recv)
                copy.start()
                sends.append(copy)

    for copy in sends:
        copy.wait_send()
    for copy in z_copies:
        copy.wait_send()
    for dz in range(4):
        for way in range(2):
            x_near(dz, way).wait_send()
            x_far(dz, way).wait_send()
        for dx in range(4):
            to_sibling(dx, dz).wait_send()
    for which in range(2):
        for i in range(1, GROUP):
            refs, to = page_copy(i, which)
            remote(refs, to, g_send.at[which, i], g_recv.at[which]).wait_send()
    arrived(key_cache, g_recv.at[0])
    arrived(value_cache, g_recv.at[1])
    arrived(att, o_recv)


def shards(queries, key_rows, value_rows, page_owner, page_slot):
    dma = pltpu.SemaphoreType.DMA
    bf16 = jnp.bfloat16
    anywhere = pl.BlockSpec(memory_space=pl.ANY)
    return pl.pallas_call(
        kernel,
        out_shape=(
            jax.ShapeDtypeStruct(queries.shape, bf16),
            jax.ShapeDtypeStruct((4, 16, 1024), bf16),
            jax.ShapeDtypeStruct((4, 16, 1024), bf16),
        ),
        in_specs=[anywhere] * 3 + [pl.BlockSpec(memory_space=pltpu.SMEM)] * 2,
        out_specs=(anywhere,) * 3,
        scratch_shapes=[
            pltpu.VMEM((2, GROUP, ROWS, HALF), bf16),
            pltpu.VMEM((GROUP, ROWS, HEAD_DIM), bf16),
            pltpu.VMEM((4, 4, 2, 512, HEAD_DIM), bf16),
            pltpu.VMEM((2, 144, SET), jnp.float32),
            pltpu.VMEM((2, 8, SET), jnp.float32),
            pltpu.VMEM((2, GROUP, ROWS, HALF), bf16),
            pltpu.VMEM((2, 32, 16, HEAD_DIM), bf16),
            dma((2, GROUP)),
            dma((2,)),
            dma((2, GROUP)),
            dma((2,)),
            dma((4,)),
            dma((4,)),
            dma((4, 4)),
            dma((4, 4)),
            dma((16,)),
            dma((16,)),
            dma((2, GROUP)),
            dma,
            dma((2, GROUP)),
            dma((2,)),
        ],
        compiler_params=pltpu.CompilerParams(
            collective_id=0, has_side_effects=True, vmem_limit_bytes=56 * 2**20
        ),
    )(queries, key_rows, value_rows, page_owner, page_slot)


def solution(mesh):
    whole = P(("ctx", "serve"), None)
    return jax.shard_map(
        shards,
        mesh=mesh,
        in_specs=(whole, whole, whole, P("ctx"), P("ctx")),
        out_specs=(whole, P(("ctx", "serve"), None, None), P(("ctx", "serve"), None, None)),
        check_vma=False,
    )
```

```python
import math

import jax
import jax.numpy as jnp
from jax import lax
from jax.experimental import pallas as pl
from jax.experimental.pallas import tpu as pltpu
from jax.sharding import PartitionSpec as P

HEAD_DIM = 128
ROWS = 32
GROUP = 8
SET = 1024
SCALE = math.log2(math.e) / math.sqrt(HEAD_DIM)
LOW = -1e30
NT = (((1,), (1,)), ((), ()))
MESH = pl.DeviceIdType.MESH


def kernel(
    q_in, k_in, v_in, owner, slot,
    att, key_cache, value_cache,
    q_land, kv_land, kv, acc, top, o_stage, pages, codes,
    kv_send, kv_recv, t_send, t_recv, q_send, q_recv, z_send, z_recv, x_send, x_recv,
    s_send, s_recv, o_send, o_recv, g_send, g_recv,
):
    ctx = lax.axis_index("ctx")
    serve = lax.axis_index("serve")
    x, z_hi = lax.div(ctx, 2), lax.rem(ctx, 2)
    z_lo, low = lax.div(serve, 8), lax.rem(serve, 8)
    y, c = lax.div(low, 2), lax.rem(low, 2)
    z = z_hi * 4 + z_lo
    side, x_odd = lax.div(x, 2), lax.rem(x, 2)
    pair = side + x_odd - 2 * side * x_odd
    x_other = x + 1 - 2 * x_odd
    xs, sides = (x, 3 - x), (side, 1 - side)
    y_odd, y_big = lax.rem(y, 2), lax.div(y, 2)
    ys = (y, y + 1 - 2 * y_odd, y + 2 - 4 * y_big, 3 - y)
    head = y * 2 + side

    def device(xx, zz, yy, cc):
        hi = lax.div(zz, 4)
        return (xx * 2 + hi, (zz - hi * 4) * 8 + yy * 2 + cc)

    def partner(i):
        xx, yy = xs[i // 4], ys[i % 4]
        return (xx * 2 + z_hi, z_lo * 8 + yy * 2 + c), sides[i // 4], yy

    sibling = (ctx, serve + 1 - 2 * c)
    z_ways = (device(x, lax.rem(z + 1, 8), y, c), device(x, lax.rem(z + 7, 8), y, c))
    across = (x_other * 2 + z_hi, serve)

    barrier = pltpu.get_barrier_semaphore()
    peers = [z_ways[0], z_ways[1], across, sibling] + [partner(i)[0] for i in range(1, GROUP)]
    for peer in peers:
        pl.semaphore_signal(barrier, inc=1, device_id=peer, device_id_type=MESH)
    pl.semaphore_wait(barrier, len(peers))

    def cols(start, size):
        return pl.ds(pl.multiple_of(start, 128), size)

    def remote(src, dst, to, send, recv):
        return pltpu.make_async_remote_copy(
            src_ref=src, dst_ref=dst, send_sem=send, recv_sem=recv,
            device_id=to, device_id_type=MESH,
        )

    def local(src, dst, sem):
        return pltpu.make_async_copy(src, dst, sem)

    def arrived(ref, sem):
        pltpu.make_async_copy(ref, ref, sem).wait()

    sends = []
    for i in range(1, GROUP):
        to, their_side, their_y = partner(i)
        for which, ref in ((0, k_in), (1, v_in)):
            src = ref.at[:, cols((their_y * 2 + their_side) * 128, 128)]
            sends.append(
                remote(src, kv_land.at[which, side, y], to, kv_send.at[which, i], kv_recv)
            )
            sends[-1].start()
    for which, ref in ((0, k_in), (1, v_in)):
        local(ref.at[:, cols(head * 128, 128)], kv_land.at[which, side, y], kv_recv).start()
    local(q_in.at[:, cols(head * 1024, 1024)], q_land.at[side, y], q_recv).start()
    for i in range(1, GROUP):
        to, their_side, their_y = partner(i)
        src = q_in.at[:, cols((their_y * 2 + their_side) * 1024, 1024)]
        sends.append(remote(src, q_land.at[side, y], to, q_send.at[i], q_recv))
        sends[-1].start()

    acc[...] = jnp.zeros_like(acc)
    top[...] = jnp.full_like(top, LOW)
    lane = lax.broadcasted_iota(jnp.int32, (8, 128), 1)
    table = jnp.zeros((8, 128), jnp.int32)
    for i in range(64):
        table = jnp.where(lane == i, owner[i] * 4 + slot[i], table)
    codes[0] = table
    sends.append(remote(codes.at[0], codes.at[1], partner(4)[0], t_send, t_recv))
    sends[-1].start()

    def z_copy(i, way, step):
        if way == 0:
            src, dst = lax.rem(8 - step, 8), 7 - step
        else:
            src, dst = step, step + 1
        if isinstance(step, int) and step == 3:
            if i == 0:
                pick = (pl.ds(way, 1),)
            else:
                pick = (2, pl.ds(way * 128, 128))
        else:
            pick = (pl.ds(0, 2),) if i == 0 else (2,)
        return remote(
            kv.at[(src, c) + pick], kv.at[(dst, c) + pick], z_ways[way],
            z_send.at[i, way, step], z_recv.at[i, way, step],
        )

    def first_cross():
        return remote(kv.at[0, c, pair], kv.at[0, c, 2], across, x_send.at[8], x_recv.at[8])

    def cross(dz):
        return remote(kv.at[dz, c, 0], kv.at[dz, c, 3], across, x_send.at[dz], x_recv.at[dz])

    def to_sibling(i, dz):
        ref = kv.at[(dz, c) + ((pl.ds(0, 2),), (2,), (3,))[i]]
        return remote(ref, ref, sibling, s_send.at[i, dz], s_recv.at[i, dz])

    def on_pair(which):
        return pl.when(pair == which)

    arrived(kv_land, kv_recv)
    for which in range(2):
        kv[0, c, which, 0:128, :] = kv_land[0, which].reshape(128, HEAD_DIM)
        kv[0, c, which, 128:256, :] = kv_land[1, which].reshape(128, HEAD_DIM).T
    first_cross().start()
    z_copy(0, 0, 0).start()
    z_copy(0, 1, 0).start()
    to_sibling(0, 0).start()

    @on_pair(1)
    def _():
        cross(0).start()

    first_cross().wait_recv()
    z_copy(1, 0, 0).start()
    z_copy(1, 1, 0).start()
    to_sibling(1, 0).start()

    @on_pair(0)
    def _():
        cross(0).wait_recv()
        to_sibling(2, 0).start()

    def attend(which, blocks):
        q = q_land[which]
        q = jnp.concatenate(
            [q[:, :, h * 128 : (h + 1) * 128].reshape(128, HEAD_DIM) for h in range(8)], axis=0
        )
        scores = []
        for role, dzs, kind in blocks:
            key = jnp.concatenate(
                [kv[dz, core, role, 0:128, :] for dz in dzs for core in range(2)], axis=0
            )
            part = lax.dot_general(key, q, NT, preferred_element_type=jnp.float32)
            if kind == "diagonal":
                row = lax.broadcasted_iota(jnp.int32, (256, 1), 0)
                key_pos = (row % 128 // 32) * 64 + (row // 128) * 32 + row % 32
                token = lax.broadcasted_iota(jnp.int32, (1, SET), 1) % 128
                query_pos = (token // 32) * 64 + c * 32 + token % 32
                part = jnp.where(key_pos <= query_pos, part, LOW)
            scores.append(part)
        old, total = top[which], acc[which]
        for (role, dzs, kind), part in zip(blocks, scores):
            if kind == "earlier":
                new, weights = old, []
                for n, dz in enumerate(dzs):
                    high = jnp.max(part[n * 256 : (n + 1) * 256], axis=0, keepdims=True)
                    new = jnp.where(z + dz >= 8, jnp.maximum(new, high), new)
                for n, dz in enumerate(dzs):
                    base = jnp.where(z + dz >= 8, new[0:1], -LOW)
                    weights.append(
                        jnp.exp2((part[n * 256 : (n + 1) * 256] - base) * SCALE).astype(jnp.bfloat16)
                    )
                weights = jnp.concatenate(weights, axis=0)
            else:
                new = jnp.maximum(old, jnp.max(part, axis=0, keepdims=True))
                weights = jnp.exp2((part - new[0:1]) * SCALE).astype(jnp.bfloat16)
            value = jnp.concatenate(
                [kv[dz, core, role, 128:256, :] for dz in dzs for core in range(2)], axis=1
            )
            value = jnp.concatenate([value, jnp.ones((16, value.shape[1]), jnp.bfloat16)], axis=0)
            product = jnp.dot(value, weights, preferred_element_type=jnp.float32)
            total = total * jnp.exp2((old - new) * SCALE)[0:1] + product
            old = new
        top[which] = old
        acc[which] = total

    def first_unit(dzs, kind):
        attend(pair, [(pair, dzs, kind)])

    def second_unit(dzs):
        attend(1, [(0, dzs, "all"), (2, dzs, "all")])

    def third_unit(dzs, kind):
        attend(1 - pair, [(3 - pair, dzs, "all"), (1 - pair, dzs, kind)])

    def place_pages():
        for which in range(2):
            code = jnp.where(side == which, codes[0], codes[1])
            spot = lax.broadcasted_iota(jnp.int32, (128, 1024), 1)
            entry = lax.broadcasted_iota(jnp.int32, (128, 1024), 0)
            page = (spot // 256) * 16 + (spot % 128 // 32) * 4 + (spot % 256 // 128) * 2 + spot % 32 // 16
            spread = jnp.where(entry == page, 1.0, 0.0).astype(jnp.bfloat16)
            token = jnp.dot(code.astype(jnp.bfloat16), spread, preferred_element_type=jnp.float32)
            token = token[0:1].astype(jnp.int32) * 16 + spot[0:1] % 16
            row = lax.broadcasted_iota(jnp.int32, (256, 1), 0)
            target = (z_lo * 8 + (row // 64) * 2 + c) * 4 + row // 16 % 4
            pick = jnp.where(target * 16 + row % 16 == token, 1.0, 0.0).astype(jnp.bfloat16)
            parts = [(lax.rem(lo + 8 - z_lo, 8), core) for lo in range(4) for core in range(2)]
            key = jnp.concatenate([kv[dz, core, which, 0:128, :] for dz, core in parts], axis=0)
            value = jnp.concatenate([kv[dz, core, which, 128:256, :] for dz, core in parts], axis=1)
            found = jnp.dot(pick, key, preferred_element_type=jnp.float32)
            pages[0, which] = found.astype(jnp.bfloat16).reshape(16, 16, HEAD_DIM)
            found = lax.dot_general(pick, value, NT, preferred_element_type=jnp.float32)
            pages[1, which] = found.astype(jnp.bfloat16).reshape(16, 16, HEAD_DIM)

    def page_copy(i, which):
        to, their_side, their_y = partner(i)
        cache = (key_cache, value_cache)[which]
        src = pages.at[which, their_side, pl.ds(their_y * 4, 4)]
        dst = cache.at[:, :, cols(head * 128, 128)]
        if i == 0:
            return local(src, dst, g_recv.at[which])
        return remote(src, dst, to, g_send.at[which, i], g_recv.at[which])

    def o_copy(which, j):
        src, dst = o_stage.at[which, ys[j]], att.at[:, cols(head * 1024, 1024)]
        xx = jnp.where(side == which, x, 3 - x)
        return src, dst, (xx * 2 + z_hi, z_lo * 8 + ys[j] * 2 + c), o_send.at[which, ys[j]]

    def finish(which):
        done = acc[which, 0:128, :] / acc[which, 128:129, :]
        for h in range(8):
            o_stage[which, :, :, h * 128 : (h + 1) * 128] = (
                done[:, h * 128 : (h + 1) * 128].T.astype(jnp.bfloat16).reshape(4, ROWS, HEAD_DIM)
            )
        for j in range(1, 4):
            src, dst, to, sem = o_copy(which, j)
            remote(src, dst, to, sem, o_recv).start()
        src, dst, to, sem = o_copy(which, 0)

        @pl.when(side == which)
        def _():
            local(src, dst, o_recv).start()

        @pl.when(side != which)
        def _():
            remote(src, dst, to, sem, o_recv).start()

    arrived(q_land, q_recv)
    to_sibling(0, 0).wait_recv()
    first_unit((0,), "diagonal")
    to_sibling(1, 0).wait_recv()
    second_unit((0,))

    @on_pair(0)
    def _():
        to_sibling(2, 0).wait_recv()

    third_unit((0,), "diagonal")

    def stage(d, carry):
        both = (8 - d, d)
        for i in range(2):
            for way in range(2):
                z_copy(i, way, d - 1).wait_recv()

                @pl.when(d < 3)
                def _():
                    z_copy(i, way, d).start()

                @pl.when(d == 3)
                def _():
                    z_copy(i, way, 3).start()

                to_sibling(i, both[way]).start()
                if i == 0:

                    @on_pair(1)
                    def _():
                        cross(both[way]).start()

        to_sibling(0, 8 - d).wait_recv()
        to_sibling(0, d).wait_recv()
        first_unit(both, "earlier")
        to_sibling(1, 8 - d).wait_recv()
        to_sibling(1, d).wait_recv()
        second_unit(both)

        @on_pair(0)
        def _():
            for dz in both:
                cross(dz).wait_recv()
                to_sibling(2, dz).start()
            for dz in both:
                to_sibling(2, dz).wait_recv()

        third_unit(both, "earlier")
        return carry

    lax.fori_loop(1, 4, stage, 0)

    z_copy(0, 0, 3).wait_recv()
    z_copy(0, 1, 3).wait_recv()
    to_sibling(0, 4).start()

    @on_pair(1)
    def _():
        cross(4).start()

    z_copy(1, 0, 3).wait_recv()
    z_copy(1, 1, 3).wait_recv()
    to_sibling(1, 4).start()
    arrived(codes.at[1], t_recv)
    place_pages()
    for which in range(2):
        for i in range(GROUP):
            page_copy(i, which).start()
    to_sibling(0, 4).wait_recv()
    first_unit((4,), "earlier")

    @on_pair(0)
    def _():
        finish(0)

    to_sibling(1, 4).wait_recv()
    second_unit((4,))

    @on_pair(1)
    def _():
        finish(1)

    @on_pair(0)
    def _():
        cross(4).wait_recv()
        to_sibling(2, 4).start()
        to_sibling(2, 4).wait_recv()

    third_unit((4,), "earlier")
    finish(1 - pair)

    for copy in sends:
        copy.wait_send()
    first_cross().wait_send()
    for way in range(2):
        for step in range(4):
            z_copy(0, way, step).wait_send()
            z_copy(1, way, step).wait_send()
    for dz in range(8):
        to_sibling(0, dz).wait_send()
        to_sibling(1, dz).wait_send()

    @on_pair(0)
    def _():
        for dz in range(8):
            to_sibling(2, dz).wait_send()

    @on_pair(1)
    def _():
        for dz in range(8):
            cross(dz).wait_send()

    for which in range(2):
        for i in range(1, GROUP):
            page_copy(i, which).wait_send()
    for which in range(2):
        for j in range(4):
            src, dst, to, sem = o_copy(which, j)
            if j == 0:

                @pl.when(side != which)
                def _():
                    remote(src, dst, to, sem, o_recv).wait_send()

            else:
                remote(src, dst, to, sem, o_recv).wait_send()
    arrived(key_cache, g_recv.at[0])
    arrived(value_cache, g_recv.at[1])
    arrived(att, o_recv)


def shards(queries, key_rows, value_rows, page_owner, page_slot):
    dma = pltpu.SemaphoreType.DMA
    bf16 = jnp.bfloat16
    anywhere = pl.BlockSpec(memory_space=pl.ANY)
    return pl.pallas_call(
        kernel,
        out_shape=(
            jax.ShapeDtypeStruct(queries.shape, bf16),
            jax.ShapeDtypeStruct((4, 16, 1024), bf16),
            jax.ShapeDtypeStruct((4, 16, 1024), bf16),
        ),
        in_specs=[anywhere] * 3 + [pl.BlockSpec(memory_space=pltpu.SMEM)] * 2,
        out_specs=(anywhere,) * 3,
        scratch_shapes=[
            pltpu.VMEM((2, 4, ROWS, SET), bf16),
            pltpu.VMEM((2, 2, 4, ROWS, HEAD_DIM), bf16),
            pltpu.VMEM((8, 2, 4, 256, HEAD_DIM), bf16),
            pltpu.VMEM((2, 144, SET), jnp.float32),
            pltpu.VMEM((2, 8, SET), jnp.float32),
            pltpu.VMEM((2, 4, ROWS, SET), bf16),
            pltpu.VMEM((2, 2, 16, 16, HEAD_DIM), bf16),
            pltpu.VMEM((2, 8, 128), jnp.int32),
            dma((2, GROUP)),
            dma,
            dma,
            dma,
            dma((GROUP,)),
            dma,
            dma((2, 2, 4)),
            dma((2, 2, 4)),
            dma((9,)),
            dma((9,)),
            dma((3, 8)),
            dma((3, 8)),
            dma((2, 4)),
            dma,
            dma((2, GROUP)),
            dma((2,)),
        ],
        compiler_params=pltpu.CompilerParams(
            collective_id=0, has_side_effects=True, vmem_limit_bytes=56 * 2**20
        ),
    )(queries, key_rows, value_rows, page_owner, page_slot)


def solution(mesh):
    whole = P(("ctx", "serve"), None)
    return jax.shard_map(
        shards,
        mesh=mesh,
        in_specs=(whole, whole, whole, P("ctx"), P("ctx")),
        out_specs=(whole, P(("ctx", "serve"), None, None), P(("ctx", "serve"), None, None)),
        check_vma=False,
    )
```

```python
import math

import jax
import jax.numpy as jnp
from jax import lax
from jax.experimental import pallas as pl
from jax.experimental.pallas import tpu as pltpu
from jax.sharding import PartitionSpec as P

HEAD_DIM = 128
ROWS = 32
GROUP = 8
SET = 1024
HALF = 512
SCALE = math.log2(math.e) / math.sqrt(HEAD_DIM)
LOW = -1e30
NT = (((1,), (1,)), ((), ()))
MESH = pl.DeviceIdType.MESH


def kernel(
    q_in, k_in, v_in, owner, slot,
    att, key_cache, value_cache,
    q_here, kv_here, q_land, kv_land, kv, acc, top, o_stage, pages, codes,
    in_sem, kv_send, kv_recv, t_send, t_recv, q_send, q_recv, z_send, z_recv, x_send, x_recv,
    s_send, s_recv, o_send, o_recv, g_send, g_recv,
):
    ctx = lax.axis_index("ctx")
    serve = lax.axis_index("serve")
    x, z_hi = lax.div(ctx, 2), lax.rem(ctx, 2)
    z_lo, low = lax.div(serve, 8), lax.rem(serve, 8)
    y, c = lax.div(low, 2), lax.rem(low, 2)
    z = z_hi * 4 + z_lo
    side, x_odd = lax.div(x, 2), lax.rem(x, 2)
    pair = side + x_odd - 2 * side * x_odd
    x_other = x + 1 - 2 * x_odd
    xs, sides = (x, 3 - x), (side, 1 - side)
    y_odd, y_big = lax.rem(y, 2), lax.div(y, 2)
    ys = (y, y + 1 - 2 * y_odd, y + 2 - 4 * y_big, 3 - y)
    head = y * 2 + side

    def device(xx, zz, yy, cc):
        hi = lax.div(zz, 4)
        return (xx * 2 + hi, (zz - hi * 4) * 8 + yy * 2 + cc)

    def partner(i):
        xx, yy = xs[i // 4], ys[i % 4]
        return (xx * 2 + z_hi, z_lo * 8 + yy * 2 + c), sides[i // 4], yy

    sibling = (ctx, serve + 1 - 2 * c)
    z_ways = (device(x, lax.rem(z + 1, 8), y, c), device(x, lax.rem(z + 7, 8), y, c))
    across = (x_other * 2 + z_hi, serve)

    loads = [
        pltpu.make_async_copy(k_in, kv_here.at[0], in_sem.at[0]),
        pltpu.make_async_copy(v_in, kv_here.at[1], in_sem.at[1]),
        pltpu.make_async_copy(q_in, q_here, in_sem.at[2]),
    ]
    barrier = pltpu.get_barrier_semaphore()
    peers = [z_ways[0], z_ways[1], across, sibling] + [partner(i)[0] for i in range(1, GROUP)]
    for peer in peers:
        pl.semaphore_signal(barrier, inc=1, device_id=peer, device_id_type=MESH)
    for load in loads:
        load.start()
    acc[...] = jnp.zeros_like(acc)
    top[...] = jnp.full_like(top, LOW)
    lane = lax.broadcasted_iota(jnp.int32, (8, 128), 1)
    table = jnp.zeros((8, 128), jnp.int32)
    for i in range(64):
        table = jnp.where(lane == i, owner[i] * 4 + slot[i], table)
    codes[0] = table
    for load in loads:
        load.wait()
    pl.semaphore_wait(barrier, len(peers))

    def cols(start, size):
        return pl.ds(pl.multiple_of(start, 128), size)

    def remote(src, dst, to, send, recv):
        return pltpu.make_async_remote_copy(
            src_ref=src, dst_ref=dst, send_sem=send, recv_sem=recv,
            device_id=to, device_id_type=MESH,
        )

    def local(src, dst, sem):
        return pltpu.make_async_copy(src, dst, sem)

    def arrived(ref, sem):
        pltpu.make_async_copy(ref, ref, sem).wait()

    sends = []
    for i in (6, 5, 7, 2, 4, 1, 3):
        to, their_side, their_y = partner(i)
        for which in range(2):
            src = kv_here.at[which, :, cols((their_y * 2 + their_side) * 128, 128)]
            sends.append(
                remote(src, kv_land.at[which, side, y], to, kv_send.at[which, i], kv_recv)
            )
            sends[-1].start()
    for which in range(2):
        src = kv_here.at[which, :, cols(head * 128, 128)]
        local(src, kv_land.at[which, side, y], kv_recv).start()
    for half in range(2):
        src = q_here.at[:, cols(head * 1024 + half * HALF, HALF)]
        local(src, q_land.at[half, side, y], q_recv.at[half]).start()
        for i in (6, 5, 7, 2, 4, 1, 3):
            to, their_side, their_y = partner(i)
            src = q_here.at[:, cols((their_y * 2 + their_side) * 1024 + half * HALF, HALF)]
            sends.append(
                remote(src, q_land.at[half, side, y], to, q_send.at[half, i], q_recv.at[half])
            )
            sends[-1].start()
    sends.append(remote(codes.at[0], codes.at[1], partner(4)[0], t_send, t_recv))
    sends[-1].start()

    def z_copy(role, way, step):
        if way == 0:
            src, dst = lax.rem(8 - step, 8), 7 - step
        else:
            src, dst = step, step + 1
        pick = (role, pl.ds(way * 128, 128)) if isinstance(step, int) and step == 3 else (role,)
        return remote(
            kv.at[(src, c) + pick], kv.at[(dst, c) + pick], z_ways[way],
            z_send.at[role, way, step], z_recv.at[role, way, step],
        )

    def first_cross():
        return remote(kv.at[0, c, 1], kv.at[0, c, 2], across, x_send.at[8], x_recv.at[8])

    def cross(dz):
        return remote(
            kv.at[dz, c, 0], kv.at[dz, c, 2 + pair], across, x_send.at[dz], x_recv.at[dz]
        )

    def to_sibling(role, dz):
        ref = kv.at[dz, c, role]
        return remote(ref, ref, sibling, s_send.at[role, dz], s_recv.at[role, dz])

    def on_pair(which):
        return pl.when(pair == which)

    def take(role, d):
        for way, dz in ((0, 8 - d), (1, d)):
            z_copy(role, way, d - 1).wait_recv()

            @pl.when(d < 3)
            def _():
                z_copy(role, way, d).start()

            @pl.when(d == 3)
            def _():
                z_copy(role, way, 3).start()

            if role == 0:
                cross(dz).start()
            to_sibling(role, dz).start()

    def take_last(role):
        z_copy(role, 0, 3).wait_recv()
        z_copy(role, 1, 3).wait_recv()
        if role == 0:
            cross(4).start()
        to_sibling(role, 4).start()

    def crossed(dzs):
        for dz in dzs:
            cross(dz).wait_recv()
            to_sibling(3 - pair, dz).start()

    def heard(roles, dzs):
        for role in roles:
            for dz in dzs:
                to_sibling(role, dz).wait_recv()

    arrived(kv_land, kv_recv)
    for which in range(2):
        kv[0, c, which, 0:128, :] = kv_land[0, which].reshape(128, HEAD_DIM)
        kv[0, c, which, 128:256, :] = kv_land[1, which].reshape(128, HEAD_DIM).T

    @on_pair(1)
    def _():
        first_cross().start()

    for role in range(2):
        z_copy(role, 0, 0).start()
        z_copy(role, 1, 0).start()
        to_sibling(role, 0).start()
        if role == 0:
            cross(0).start()

    @on_pair(0)
    def _():
        first_cross().wait_recv()
        z_copy(2, 0, 0).start()
        z_copy(2, 1, 0).start()
        to_sibling(2, 0).start()

    crossed((0,))

    def queries_of(which, heads):
        parts = []
        for h in heads:
            q = q_land[h // 4, which, :, :, h % 4 * 128 : (h % 4 + 1) * 128]
            parts.append(q.reshape(128, HEAD_DIM))
        return jnp.concatenate(parts, axis=0)

    def attend(which, heads, blocks):
        q = queries_of(which, heads)
        spot = slice(heads[0] * 128, heads[-1] * 128 + 128)
        scores = []
        for role, dzs, kind in blocks:
            key = jnp.concatenate(
                [kv[dz, core, role, 0:128, :] for dz in dzs for core in range(2)], axis=0
            )
            part = lax.dot_general(key, q, NT, preferred_element_type=jnp.float32)
            if kind == "diagonal":
                row = lax.broadcasted_iota(jnp.int32, (256, 1), 0)
                key_pos = (row % 128 // 32) * 64 + (row // 128) * 32 + row % 32
                token = lax.broadcasted_iota(jnp.int32, (1, q.shape[0]), 1) % 128
                query_pos = (token // 32) * 64 + c * 32 + token % 32
                part = jnp.where(key_pos <= query_pos, part, LOW)
            scores.append(part)
        old, total = top[which, :, spot], acc[which, :, spot]
        for (role, dzs, kind), part in zip(blocks, scores):
            if kind == "earlier":
                new, weights = old, []
                for n, dz in enumerate(dzs):
                    high = jnp.max(part[n * 256 : (n + 1) * 256], axis=0, keepdims=True)
                    new = jnp.where(z + dz >= 8, jnp.maximum(new, high), new)
                for n, dz in enumerate(dzs):
                    base = jnp.where(z + dz >= 8, new[0:1], -LOW)
                    weights.append(
                        jnp.exp2((part[n * 256 : (n + 1) * 256] - base) * SCALE).astype(jnp.bfloat16)
                    )
                weights = jnp.concatenate(weights, axis=0)
            else:
                new = jnp.maximum(old, jnp.max(part, axis=0, keepdims=True))
                weights = jnp.exp2((part - new[0:1]) * SCALE).astype(jnp.bfloat16)
            value = jnp.concatenate(
                [kv[dz, core, role, 128:256, :] for dz in dzs for core in range(2)], axis=1
            )
            value = jnp.concatenate([value, jnp.ones((16, value.shape[1]), jnp.bfloat16)], axis=0)
            product = jnp.dot(value, weights, preferred_element_type=jnp.float32)
            total = total * jnp.exp2((old - new) * SCALE)[0:1] + product
            old = new
        top[which, :, spot] = old
        acc[which, :, spot] = total

    def own_units(heads, dzs, kind):
        attend(1, heads, [(0, dzs, "all"), (1, dzs, kind)])
        attend(0, heads, [(0, dzs, kind)])

    def other_units(heads, dzs):
        @on_pair(0)
        def _():
            attend(1, heads, [(2, dzs, "all"), (3, dzs, "all")])

        @on_pair(1)
        def _():
            attend(1, heads, [(2, dzs, "all")])
            attend(0, heads, [(2, dzs, "all")])

    everything = range(8)
    halves = (range(4), range(4, 8))

    def place_pages():
        for which in range(2):
            code = jnp.where(side == which, codes[0], codes[1])
            spot = lax.broadcasted_iota(jnp.int32, (128, 1024), 1)
            entry = lax.broadcasted_iota(jnp.int32, (128, 1024), 0)
            page = (spot // 256) * 16 + (spot % 128 // 32) * 4 + (spot % 256 // 128) * 2 + spot % 32 // 16
            spread = jnp.where(entry == page, 1.0, 0.0).astype(jnp.bfloat16)
            token = jnp.dot(code.astype(jnp.bfloat16), spread, preferred_element_type=jnp.float32)
            token = token[0:1].astype(jnp.int32) * 16 + spot[0:1] % 16
            row = lax.broadcasted_iota(jnp.int32, (256, 1), 0)
            target = (z_lo * 8 + (row // 64) * 2 + c) * 4 + row // 16 % 4
            pick = jnp.where(target * 16 + row % 16 == token, 1.0, 0.0).astype(jnp.bfloat16)
            parts = [(lax.rem(lo + 8 - z_lo, 8), core) for lo in range(4) for core in range(2)]
            key = jnp.concatenate([kv[dz, core, which, 0:128, :] for dz, core in parts], axis=0)
            value = jnp.concatenate([kv[dz, core, which, 128:256, :] for dz, core in parts], axis=1)
            found = jnp.dot(pick, key, preferred_element_type=jnp.float32)
            pages[0, which] = found.astype(jnp.bfloat16).reshape(16, 16, HEAD_DIM)
            found = lax.dot_general(pick, value, NT, preferred_element_type=jnp.float32)
            pages[1, which] = found.astype(jnp.bfloat16).reshape(16, 16, HEAD_DIM)

    def page_copy(i, which):
        to, their_side, their_y = partner(i)
        cache = (key_cache, value_cache)[which]
        src = pages.at[which, their_side, pl.ds(their_y * 4, 4)]
        dst = cache.at[:, :, cols(head * 128, 128)]
        if i == 0:
            return local(src, dst, g_recv.at[which])
        return remote(src, dst, to, g_send.at[which, i], g_recv.at[which])

    def o_copy(which, half, j):
        src = o_stage.at[which, half, ys[j]]
        dst = att.at[:, cols(head * 1024 + half * HALF, HALF)]
        xx = jnp.where(side == which, x, 3 - x)
        to = (xx * 2 + z_hi, z_lo * 8 + ys[j] * 2 + c)
        return src, dst, to, o_send.at[which, half, ys[j]]

    def finish(which, half):
        done = acc[which, 0:128, half * 512 : (half + 1) * 512]
        done = done / acc[which, 128:129, half * 512 : (half + 1) * 512]
        for h in range(4):
            o_stage[which, half, :, :, h * 128 : (h + 1) * 128] = (
                done[:, h * 128 : (h + 1) * 128].T.astype(jnp.bfloat16).reshape(4, ROWS, HEAD_DIM)
            )

    def send_finished(which, half):
        for j in (2, 1, 3):
            src, dst, to, sem = o_copy(which, half, j)
            remote(src, dst, to, sem, o_recv).start()
        src, dst, to, sem = o_copy(which, half, 0)

        @pl.when(side == which)
        def _():
            local(src, dst, o_recv).start()

        @pl.when(side != which)
        def _():
            remote(src, dst, to, sem, o_recv).start()

    heard((0, 1), (0,))
    arrived(q_land.at[0], q_recv.at[0])
    own_units(halves[0], (0,), "diagonal")
    take(0, 1)
    take(1, 1)
    heard((2,), (0,))

    @on_pair(0)
    def _():
        heard((3,), (0,))

    other_units(halves[0], (0,))
    arrived(q_land.at[1], q_recv.at[1])
    own_units(halves[1], (0,), "diagonal")
    other_units(halves[1], (0,))

    def stage(d, carry):
        both = (8 - d, d)

        @on_pair(0)
        def _():
            take(2, d)

        heard((0, 1), both)
        own_units(everything, both, "earlier")
        crossed(both)

        @pl.when(d < 3)
        def _():
            take(0, d + 1)
            take(1, d + 1)

        @pl.when(d == 3)
        def _():
            take_last(0)
            take_last(1)
            arrived(codes.at[1], t_recv)
            place_pages()
            for which in range(2):
                for i in range(GROUP):
                    page_copy(i, which).start()

        heard((2,), both)

        @on_pair(0)
        def _():
            heard((3,), both)

        other_units(everything, both)
        return carry

    lax.fori_loop(1, 4, stage, 0)

    @on_pair(0)
    def _():
        take_last(2)

    heard((0, 1), (4,))
    own_units(halves[0], (4,), "earlier")
    crossed((4,))
    own_units(halves[1], (4,), "earlier")
    heard((2,), (4,))

    @on_pair(0)
    def _():
        heard((3,), (4,))

    for half in range(2):
        other_units(halves[half], (4,))
        for which in range(2):
            finish(which, half)
        for which in range(2):
            send_finished(which, half)

    for copy in sends:
        copy.wait_send()
    for role in range(2):
        for way in range(2):
            for step in range(4):
                z_copy(role, way, step).wait_send()
    for dz in range(8):
        cross(dz).wait_send()
        for role in range(3):
            to_sibling(role, dz).wait_send()

    @on_pair(0)
    def _():
        for way in range(2):
            for step in range(4):
                z_copy(2, way, step).wait_send()
        for dz in range(8):
            to_sibling(3, dz).wait_send()

    @on_pair(1)
    def _():
        first_cross().wait_send()

    for which in range(2):
        for i in range(1, GROUP):
            page_copy(i, which).wait_send()
    for which in range(2):
        for half in range(2):
            for j in range(1, 4):
                src, dst, to, sem = o_copy(which, half, j)
                remote(src, dst, to, sem, o_recv).wait_send()

        @pl.when(side != which)
        def _():
            for half in range(2):
                src, dst, to, sem = o_copy(which, half, 0)
                remote(src, dst, to, sem, o_recv).wait_send()

    arrived(key_cache, g_recv.at[0])
    arrived(value_cache, g_recv.at[1])
    arrived(att, o_recv)


def move(att, key_cache, value_cache, att_out, key_out, value_out):
    att_out[...] = att[...]
    key_out[...] = key_cache[...]
    value_out[...] = value_cache[...]


def shards(queries, key_rows, value_rows, page_owner, page_slot):
    dma = pltpu.SemaphoreType.DMA
    bf16 = jnp.bfloat16
    anywhere = pl.BlockSpec(memory_space=pl.ANY)
    held = pl.pallas_call(
        kernel,
        out_shape=(
            jax.ShapeDtypeStruct(queries.shape, bf16),
            jax.ShapeDtypeStruct((4, 16, 1024), bf16),
            jax.ShapeDtypeStruct((4, 16, 1024), bf16),
        ),
        in_specs=[anywhere] * 3 + [pl.BlockSpec(memory_space=pltpu.SMEM)] * 2,
        out_specs=(anywhere,) * 3,
        scratch_shapes=[
            pltpu.VMEM((ROWS, 8192), bf16),
            pltpu.VMEM((2, ROWS, 1024), bf16),
            pltpu.VMEM((2, 2, 4, ROWS, HALF), bf16),
            pltpu.VMEM((2, 2, 4, ROWS, HEAD_DIM), bf16),
            pltpu.VMEM((8, 2, 4, 256, HEAD_DIM), bf16),
            pltpu.VMEM((2, 144, SET), jnp.float32),
            pltpu.VMEM((2, 8, SET), jnp.float32),
            pltpu.VMEM((2, 2, 4, ROWS, HALF), bf16),
            pltpu.VMEM((2, 2, 16, 16, HEAD_DIM), bf16),
            pltpu.VMEM((2, 8, 128), jnp.int32),
            dma((3,)),
            dma((2, GROUP)),
            dma,
            dma,
            dma,
            dma((2, GROUP)),
            dma((2,)),
            dma((3, 2, 4)),
            dma((3, 2, 4)),
            dma((9,)),
            dma((9,)),
            dma((4, 8)),
            dma((4, 8)),
            dma((2, 2, 4)),
            dma,
            dma((2, GROUP)),
            dma((2,)),
        ],
        compiler_params=pltpu.CompilerParams(
            collective_id=0, has_side_effects=True, vmem_limit_bytes=56 * 2**20
        ),
    )(queries, key_rows, value_rows, page_owner, page_slot)
    return pl.pallas_call(
        move,
        out_shape=tuple(jax.ShapeDtypeStruct(a.shape, bf16) for a in held),
        in_specs=[pl.BlockSpec(memory_space=pltpu.VMEM)] * 3,
        out_specs=(pl.BlockSpec(memory_space=pltpu.VMEM),) * 3,
    )(*held)


def solution(mesh):
    whole = P(("ctx", "serve"), None)
    return jax.shard_map(
        shards,
        mesh=mesh,
        in_specs=(whole, whole, whole, P("ctx"), P("ctx")),
        out_specs=(whole, P(("ctx", "serve"), None, None), P(("ctx", "serve"), None, None)),
        check_vma=False,
    )
```

```python
import math

import jax
import jax.numpy as jnp
from jax import lax
from jax.experimental import pallas as pl
from jax.experimental.pallas import tpu as pltpu
from jax.sharding import PartitionSpec as P

HEAD_DIM = 128
ROWS = 32
GROUP = 8
SET = 1024
HALF = 512
SCALE = math.log2(math.e) / math.sqrt(HEAD_DIM)
LOW = -1e30
NT = (((1,), (1,)), ((), ()))
MESH = pl.DeviceIdType.MESH


def kernel(
    q_in, k_in, v_in, owner, slot,
    att, key_cache, value_cache,
    q_here, kv_here, q_land, kv_land, kv, acc, top, o_stage, pages, codes,
    in_sem, kv_send, kv_recv, t_send, t_recv, q_send, q_recv, z_send, z_recv, x_send, x_recv,
    s_send, s_recv, o_send, o_recv, g_send, g_recv,
):
    ctx = lax.axis_index("ctx")
    serve = lax.axis_index("serve")
    x, z_hi = lax.div(ctx, 2), lax.rem(ctx, 2)
    z_lo, low = lax.div(serve, 8), lax.rem(serve, 8)
    y, c = lax.div(low, 2), lax.rem(low, 2)
    z = z_hi * 4 + z_lo
    side, x_odd = lax.div(x, 2), lax.rem(x, 2)
    pair = side + x_odd - 2 * side * x_odd
    x_other = x + 1 - 2 * x_odd
    xs, sides = (x, 3 - x), (side, 1 - side)
    y_odd, y_big = lax.rem(y, 2), lax.div(y, 2)
    ys = (y, y + 1 - 2 * y_odd, y + 2 - 4 * y_big, 3 - y)
    head = y * 2 + side

    def device(xx, zz, yy, cc):
        hi = lax.div(zz, 4)
        return (xx * 2 + hi, (zz - hi * 4) * 8 + yy * 2 + cc)

    def partner(i):
        xx, yy = xs[i // 4], ys[i % 4]
        return (xx * 2 + z_hi, z_lo * 8 + yy * 2 + c), sides[i // 4], yy

    sibling = (ctx, serve + 1 - 2 * c)
    z_ways = (device(x, lax.rem(z + 1, 8), y, c), device(x, lax.rem(z + 7, 8), y, c))
    across = (x_other * 2 + z_hi, serve)

    loads = [
        pltpu.make_async_copy(k_in, kv_here.at[0], in_sem.at[0]),
        pltpu.make_async_copy(v_in, kv_here.at[1], in_sem.at[1]),
        pltpu.make_async_copy(q_in, q_here, in_sem.at[2]),
    ]
    barrier = pltpu.get_barrier_semaphore()
    peers = [z_ways[0], z_ways[1], across, sibling] + [partner(i)[0] for i in range(1, GROUP)]
    for peer in peers:
        pl.semaphore_signal(barrier, inc=1, device_id=peer, device_id_type=MESH)
    for load in loads:
        load.start()
    acc[...] = jnp.zeros_like(acc)
    top[...] = jnp.full_like(top, LOW)
    lane = lax.broadcasted_iota(jnp.int32, (8, 128), 1)
    table = jnp.zeros((8, 128), jnp.int32)
    for i in range(64):
        table = jnp.where(lane == i, owner[i] * 4 + slot[i], table)
    codes[0] = table
    for load in loads:
        load.wait()
    pl.semaphore_wait(barrier, len(peers))

    def cols(start, size):
        return pl.ds(pl.multiple_of(start, 128), size)

    def remote(src, dst, to, send, recv):
        return pltpu.make_async_remote_copy(
            src_ref=src, dst_ref=dst, send_sem=send, recv_sem=recv,
            device_id=to, device_id_type=MESH,
        )

    def local(src, dst, sem):
        return pltpu.make_async_copy(src, dst, sem)

    def arrived(ref, sem):
        pltpu.make_async_copy(ref, ref, sem).wait()

    sends = []
    for i in (6, 5, 7, 2, 4, 1, 3):
        to, their_side, their_y = partner(i)
        src = kv_here.at[:, :, cols((their_y * 2 + their_side) * 128, 128)]
        sends.append(remote(src, kv_land.at[:, side, y], to, kv_send.at[i], kv_recv))
        sends[-1].start()
    local(kv_here.at[:, :, cols(head * 128, 128)], kv_land.at[:, side, y], kv_recv).start()
    for half in range(2):
        src = q_here.at[:, cols(head * 1024 + half * HALF, HALF)]
        local(src, q_land.at[half, side, y], q_recv.at[half]).start()
        for i in (6, 5, 7, 2, 4, 1, 3):
            to, their_side, their_y = partner(i)
            src = q_here.at[:, cols((their_y * 2 + their_side) * 1024 + half * HALF, HALF)]
            sends.append(
                remote(src, q_land.at[half, side, y], to, q_send.at[half, i], q_recv.at[half])
            )
            sends[-1].start()
    sends.append(remote(codes.at[0], codes.at[1], partner(4)[0], t_send, t_recv))
    sends[-1].start()

    def z_copy(role, way, step):
        src, dst = ((8 - step) % 8, 7 - step) if way == 0 else (step, step + 1)
        pick = (role,) if step < 3 else (role, pl.ds(way * 128, 128))
        return remote(
            kv.at[(src, c) + pick], kv.at[(dst, c) + pick], z_ways[way],
            z_send.at[role, way, step], z_recv.at[role, way, step],
        )

    def first_cross():
        return remote(kv.at[0, c, 1], kv.at[0, c, 2], across, x_send.at[8], x_recv.at[8])

    def cross(dz):
        return remote(
            kv.at[dz, c, 0], kv.at[dz, c, 2 + pair], across, x_send.at[dz], x_recv.at[dz]
        )

    def to_sibling(role, dz):
        ref = kv.at[dz, c, role]
        return remote(ref, ref, sibling, s_send.at[role, dz], s_recv.at[role, dz])

    def on_pair(which):
        return pl.when(pair == which)

    def take(role, d):
        if d < 4:
            for way, dz in ((0, 8 - d), (1, d)):
                z_copy(role, way, d - 1).wait_recv()
                z_copy(role, way, d).start()
                if role == 0:
                    cross(dz).start()
                to_sibling(role, dz).start()
        else:
            z_copy(role, 0, 3).wait_recv()
            z_copy(role, 1, 3).wait_recv()
            if role == 0:
                cross(4).start()
            to_sibling(role, 4).start()

    def crossed(dzs):
        for dz in dzs:
            cross(dz).wait_recv()
            to_sibling(3 - pair, dz).start()

    def heard(roles, dzs):
        for role in roles:
            for dz in dzs:
                to_sibling(role, dz).wait_recv()

    arrived(kv_land, kv_recv)
    for which in range(2):
        kv[0, c, which, 0:128, :] = kv_land[0, which].reshape(128, HEAD_DIM)
        kv[0, c, which, 128:256, :] = kv_land[1, which].reshape(128, HEAD_DIM).T

    @on_pair(1)
    def _():
        first_cross().start()

    for role in range(2):
        z_copy(role, 0, 0).start()
        z_copy(role, 1, 0).start()
        to_sibling(role, 0).start()
        if role == 0:
            cross(0).start()

    @on_pair(0)
    def _():
        first_cross().wait_recv()
        z_copy(2, 0, 0).start()
        z_copy(2, 1, 0).start()
        to_sibling(2, 0).start()

    crossed((0,))

    def queries_of(which, heads):
        parts = []
        for h in heads:
            q = q_land[h // 4, which, :, :, h % 4 * 128 : (h % 4 + 1) * 128]
            parts.append(q.reshape(128, HEAD_DIM))
        return jnp.concatenate(parts, axis=0)

    def attend(which, heads, blocks):
        q = queries_of(which, heads)
        spot = slice(heads[0] * 128, heads[-1] * 128 + 128)
        scores = []
        for role, dzs, kind in blocks:
            key = jnp.concatenate(
                [kv[dz, core, role, 0:128, :] for dz in dzs for core in range(2)], axis=0
            )
            part = lax.dot_general(key, q, NT, preferred_element_type=jnp.float32)
            if kind == "diagonal":
                row = lax.broadcasted_iota(jnp.int32, (256, 1), 0)
                key_pos = (row % 128 // 32) * 64 + (row // 128) * 32 + row % 32
                token = lax.broadcasted_iota(jnp.int32, (1, q.shape[0]), 1) % 128
                query_pos = (token // 32) * 64 + c * 32 + token % 32
                part = jnp.where(key_pos <= query_pos, part, LOW)
            scores.append(part)
        old, total = top[which, :, spot], acc[which, :, spot]
        for (role, dzs, kind), part in zip(blocks, scores):
            if kind == "earlier":
                new, weights = old, []
                for n, dz in enumerate(dzs):
                    high = jnp.max(part[n * 256 : (n + 1) * 256], axis=0, keepdims=True)
                    new = jnp.where(z + dz >= 8, jnp.maximum(new, high), new)
                for n, dz in enumerate(dzs):
                    base = jnp.where(z + dz >= 8, new[0:1], -LOW)
                    weights.append(
                        jnp.exp2((part[n * 256 : (n + 1) * 256] - base) * SCALE).astype(jnp.bfloat16)
                    )
                weights = jnp.concatenate(weights, axis=0)
            else:
                new = jnp.maximum(old, jnp.max(part, axis=0, keepdims=True))
                weights = jnp.exp2((part - new[0:1]) * SCALE).astype(jnp.bfloat16)
            value = jnp.concatenate(
                [kv[dz, core, role, 128:256, :] for dz in dzs for core in range(2)], axis=1
            )
            value = jnp.concatenate([value, jnp.ones((16, value.shape[1]), jnp.bfloat16)], axis=0)
            product = jnp.dot(value, weights, preferred_element_type=jnp.float32)
            total = total * jnp.exp2((old - new) * SCALE)[0:1] + product
            old = new
        top[which, :, spot] = old
        acc[which, :, spot] = total

    def own_units(heads, dzs, kind):
        attend(1, heads, [(0, dzs, "all"), (1, dzs, kind)])
        attend(0, heads, [(0, dzs, kind)])

    def other_units(heads, dzs):
        @on_pair(0)
        def _():
            attend(1, heads, [(2, dzs, "all"), (3, dzs, "all")])

        @on_pair(1)
        def _():
            attend(1, heads, [(2, dzs, "all")])
            attend(0, heads, [(2, dzs, "all")])

    everything = range(8)
    halves = (range(4), range(4, 8))

    def place_pages():
        for which in range(2):
            code = jnp.where(side == which, codes[0], codes[1])
            spot = lax.broadcasted_iota(jnp.int32, (128, 1024), 1)
            entry = lax.broadcasted_iota(jnp.int32, (128, 1024), 0)
            page = (spot // 256) * 16 + (spot % 128 // 32) * 4 + (spot % 256 // 128) * 2 + spot % 32 // 16
            spread = jnp.where(entry == page, 1.0, 0.0).astype(jnp.bfloat16)
            token = jnp.dot(code.astype(jnp.bfloat16), spread, preferred_element_type=jnp.float32)
            token = token[0:1].astype(jnp.int32) * 16 + spot[0:1] % 16
            row = lax.broadcasted_iota(jnp.int32, (256, 1), 0)
            target = (z_lo * 8 + (row // 64) * 2 + c) * 4 + row // 16 % 4
            pick = jnp.where(target * 16 + row % 16 == token, 1.0, 0.0).astype(jnp.bfloat16)
            parts = [(lax.rem(lo + 8 - z_lo, 8), core) for lo in range(4) for core in range(2)]
            key = jnp.concatenate([kv[dz, core, which, 0:128, :] for dz, core in parts], axis=0)
            value = jnp.concatenate([kv[dz, core, which, 128:256, :] for dz, core in parts], axis=1)
            found = jnp.dot(pick, key, preferred_element_type=jnp.float32)
            pages[0, which] = found.astype(jnp.bfloat16).reshape(16, 16, HEAD_DIM)
            found = lax.dot_general(pick, value, NT, preferred_element_type=jnp.float32)
            pages[1, which] = found.astype(jnp.bfloat16).reshape(16, 16, HEAD_DIM)

    def page_copy(i, which):
        to, their_side, their_y = partner(i)
        cache = (key_cache, value_cache)[which]
        src = pages.at[which, their_side, pl.ds(their_y * 4, 4)]
        dst = cache.at[:, :, cols(head * 128, 128)]
        if i == 0:
            return local(src, dst, g_recv.at[which])
        return remote(src, dst, to, g_send.at[which, i], g_recv.at[which])

    def o_copy(which, half, j):
        src = o_stage.at[which, half, ys[j]]
        dst = att.at[:, cols(head * 1024 + half * HALF, HALF)]
        xx = jnp.where(side == which, x, 3 - x)
        to = (xx * 2 + z_hi, z_lo * 8 + ys[j] * 2 + c)
        return src, dst, to, o_send.at[which, half, ys[j]]

    def finish(which, half):
        done = acc[which, 0:128, half * 512 : (half + 1) * 512]
        done = done / acc[which, 128:129, half * 512 : (half + 1) * 512]
        for h in range(4):
            o_stage[which, half, :, :, h * 128 : (h + 1) * 128] = (
                done[:, h * 128 : (h + 1) * 128].T.astype(jnp.bfloat16).reshape(4, ROWS, HEAD_DIM)
            )

    def send_finished(which, half):
        for j in (2, 1, 3):
            src, dst, to, sem = o_copy(which, half, j)
            remote(src, dst, to, sem, o_recv).start()
        src, dst, to, sem = o_copy(which, half, 0)

        @pl.when(side == which)
        def _():
            local(src, dst, o_recv).start()

        @pl.when(side != which)
        def _():
            remote(src, dst, to, sem, o_recv).start()

    heard((0, 1), (0,))
    arrived(q_land.at[0], q_recv.at[0])
    own_units(halves[0], (0,), "diagonal")
    take(0, 1)
    take(1, 1)
    heard((2,), (0,))

    @on_pair(0)
    def _():
        heard((3,), (0,))

    other_units(halves[0], (0,))

    @on_pair(0)
    def _():
        take(2, 1)

    arrived(q_land.at[1], q_recv.at[1])
    own_units(halves[1], (0,), "diagonal")
    other_units(halves[1], (0,))

    for d in range(1, 4):
        both = (8 - d, d)
        take(0, d + 1)
        crossed(both)
        heard((0, 1), both)
        own_units(everything, both, "earlier")
        take(1, d + 1)

        @on_pair(0)
        def _():
            take(2, d + 1)

        if d == 3:
            arrived(codes.at[1], t_recv)
            place_pages()
            for which in range(2):
                for i in range(GROUP):
                    page_copy(i, which).start()
        heard((2,), both)

        @on_pair(0)
        def _():
            heard((3,), both)

        other_units(everything, both)

    crossed((4,))
    heard((0, 1), (4,))
    for half in range(2):
        own_units(halves[half], (4,), "earlier")

    @on_pair(0)
    def _():
        for half in range(2):
            finish(0, half)
            send_finished(0, half)

    heard((2,), (4,))

    @on_pair(0)
    def _():
        heard((3,), (4,))
        for half in range(2):
            attend(1, halves[half], [(2, (4,), "all"), (3, (4,), "all")])
            finish(1, half)
            send_finished(1, half)

    @on_pair(1)
    def _():
        for which in (1, 0):
            for half in range(2):
                attend(which, halves[half], [(2, (4,), "all")])
                finish(which, half)
                send_finished(which, half)

    for copy in sends:
        copy.wait_send()
    for role in range(2):
        for way in range(2):
            for step in range(4):
                z_copy(role, way, step).wait_send()
    for dz in range(8):
        cross(dz).wait_send()
        for role in range(3):
            to_sibling(role, dz).wait_send()

    @on_pair(0)
    def _():
        for way in range(2):
            for step in range(4):
                z_copy(2, way, step).wait_send()
        for dz in range(8):
            to_sibling(3, dz).wait_send()

    @on_pair(1)
    def _():
        first_cross().wait_send()

    for which in range(2):
        for i in range(1, GROUP):
            page_copy(i, which).wait_send()
    for which in range(2):
        for half in range(2):
            for j in range(1, 4):
                src, dst, to, sem = o_copy(which, half, j)
                remote(src, dst, to, sem, o_recv).wait_send()

        @pl.when(side != which)
        def _():
            for half in range(2):
                src, dst, to, sem = o_copy(which, half, 0)
                remote(src, dst, to, sem, o_recv).wait_send()

    arrived(key_cache, g_recv.at[0])
    arrived(value_cache, g_recv.at[1])
    arrived(att, o_recv)


def move(att, key_cache, value_cache, att_out, key_out, value_out, held, held_key, held_value, sem):
    parts = [(key_cache, held_key, key_out), (value_cache, held_value, value_out)]
    for n in range(4):
        columns = pl.ds(n * 2048, 2048)
        parts.append((att.at[:, columns], held.at[:, columns], att_out.at[:, columns]))
    loads = [pltpu.make_async_copy(src, at, sem.at[0, n]) for n, (src, at, _) in enumerate(parts)]
    stores = [pltpu.make_async_copy(at, dst, sem.at[1, n]) for n, (_, at, dst) in enumerate(parts)]
    for load in loads:
        load.start()
    for load, store in zip(loads, stores):
        load.wait()
        store.start()
    for store in stores:
        store.wait()


def shards(queries, key_rows, value_rows, page_owner, page_slot):
    dma = pltpu.SemaphoreType.DMA
    bf16 = jnp.bfloat16
    anywhere = pl.BlockSpec(memory_space=pl.ANY)
    held = pl.pallas_call(
        kernel,
        out_shape=(
            jax.ShapeDtypeStruct(queries.shape, bf16),
            jax.ShapeDtypeStruct((4, 16, 1024), bf16),
            jax.ShapeDtypeStruct((4, 16, 1024), bf16),
        ),
        in_specs=[anywhere] * 3 + [pl.BlockSpec(memory_space=pltpu.SMEM)] * 2,
        out_specs=(anywhere,) * 3,
        scratch_shapes=[
            pltpu.VMEM((ROWS, 8192), bf16),
            pltpu.VMEM((2, ROWS, 1024), bf16),
            pltpu.VMEM((2, 2, 4, ROWS, HALF), bf16),
            pltpu.VMEM((2, 2, 4, ROWS, HEAD_DIM), bf16),
            pltpu.VMEM((8, 2, 4, 256, HEAD_DIM), bf16),
            pltpu.VMEM((2, 144, SET), jnp.float32),
            pltpu.VMEM((2, 8, SET), jnp.float32),
            pltpu.VMEM((2, 2, 4, ROWS, HALF), bf16),
            pltpu.VMEM((2, 2, 16, 16, HEAD_DIM), bf16),
            pltpu.VMEM((2, 8, 128), jnp.int32),
            dma((3,)),
            dma((GROUP,)),
            dma,
            dma,
            dma,
            dma((2, GROUP)),
            dma((2,)),
            dma((3, 2, 4)),
            dma((3, 2, 4)),
            dma((9,)),
            dma((9,)),
            dma((4, 8)),
            dma((4, 8)),
            dma((2, 2, 4)),
            dma,
            dma((2, GROUP)),
            dma((2,)),
        ],
        compiler_params=pltpu.CompilerParams(
            collective_id=0, has_side_effects=True, vmem_limit_bytes=56 * 2**20
        ),
    )(queries, key_rows, value_rows, page_owner, page_slot)
    return pl.pallas_call(
        move,
        out_shape=tuple(jax.ShapeDtypeStruct(a.shape, bf16) for a in held),
        in_specs=[anywhere] * 3,
        out_specs=(anywhere,) * 3,
        scratch_shapes=[pltpu.VMEM(a.shape, bf16) for a in held] + [dma((2, 6))],
    )(*held)


def solution(mesh):
    whole = P(("ctx", "serve"), None)
    return jax.shard_map(
        shards,
        mesh=mesh,
        in_specs=(whole, whole, whole, P("ctx"), P("ctx")),
        out_specs=(whole, P(("ctx", "serve"), None, None), P(("ctx", "serve"), None, None)),
        check_vma=False,
    )
```

```python
import math

import jax
import jax.numpy as jnp
from jax import lax
from jax.experimental import pallas as pl
from jax.experimental.pallas import tpu as pltpu
from jax.sharding import PartitionSpec as P

HEAD_DIM = 128
ROWS = 32
GROUP = 8
SET = 1024
HALF = 512
SCALE = math.log2(math.e) / math.sqrt(HEAD_DIM)
LOW = -1e30
NT = (((1,), (1,)), ((), ()))
MESH = pl.DeviceIdType.MESH


def kernel(
    q_in, k_in, v_in, owner, slot,
    att, key_cache, value_cache,
    q_here, kv_here, q_land, kv_land, kv, acc, top, o_stage, pages, codes,
    in_sem, kv_send, kv_recv, t_send, t_recv, q_send, q_recv, z_send, z_recv, x_send, x_recv,
    s_send, s_recv, o_send, o_recv, g_send, g_recv,
):
    ctx = lax.axis_index("ctx")
    serve = lax.axis_index("serve")
    x, z_hi = lax.div(ctx, 2), lax.rem(ctx, 2)
    z_lo, low = lax.div(serve, 8), lax.rem(serve, 8)
    y, c = lax.div(low, 2), lax.rem(low, 2)
    z = z_hi * 4 + z_lo
    side, x_odd = lax.div(x, 2), lax.rem(x, 2)
    pair = side + x_odd - 2 * side * x_odd
    x_other = x + 1 - 2 * x_odd
    xs, sides = (x, 3 - x), (side, 1 - side)
    y_odd, y_big = lax.rem(y, 2), lax.div(y, 2)
    ys = (y, y + 1 - 2 * y_odd, y + 2 - 4 * y_big, 3 - y)
    head = y * 2 + side

    def device(xx, zz, yy, cc):
        hi = lax.div(zz, 4)
        return (xx * 2 + hi, (zz - hi * 4) * 8 + yy * 2 + cc)

    def partner(i):
        xx, yy = xs[i // 4], ys[i % 4]
        return (xx * 2 + z_hi, z_lo * 8 + yy * 2 + c), sides[i // 4], yy

    sibling = (ctx, serve + 1 - 2 * c)
    z_ways = (device(x, lax.rem(z + 1, 8), y, c), device(x, lax.rem(z + 7, 8), y, c))
    across = (x_other * 2 + z_hi, serve)

    loads = [
        pltpu.make_async_copy(k_in, kv_here.at[0], in_sem.at[0]),
        pltpu.make_async_copy(v_in, kv_here.at[1], in_sem.at[1]),
        pltpu.make_async_copy(q_in, q_here, in_sem.at[2]),
    ]
    barrier = pltpu.get_barrier_semaphore()
    peers = [z_ways[0], z_ways[1], across, sibling] + [partner(i)[0] for i in range(1, GROUP)]
    for peer in peers:
        pl.semaphore_signal(barrier, inc=1, device_id=peer, device_id_type=MESH)
    for load in loads:
        load.start()
    acc[...] = jnp.zeros_like(acc)
    top[...] = jnp.full_like(top, LOW)
    lane = lax.broadcasted_iota(jnp.int32, (8, 128), 1)
    table = jnp.zeros((8, 128), jnp.int32)
    for i in range(64):
        table = jnp.where(lane == i, owner[i] * 4 + slot[i], table)
    codes[0] = table
    for load in loads:
        load.wait()
    pl.semaphore_wait(barrier, len(peers))

    def cols(start, size):
        return pl.ds(pl.multiple_of(start, 128), size)

    def remote(src, dst, to, send, recv):
        return pltpu.make_async_remote_copy(
            src_ref=src, dst_ref=dst, send_sem=send, recv_sem=recv,
            device_id=to, device_id_type=MESH,
        )

    def local(src, dst, sem):
        return pltpu.make_async_copy(src, dst, sem)

    def arrived(ref, sem):
        pltpu.make_async_copy(ref, ref, sem).wait()

    sends = []
    for i in (6, 5, 7, 2, 4, 1, 3):
        to, their_side, their_y = partner(i)
        src = kv_here.at[:, :, cols((their_y * 2 + their_side) * 128, 128)]
        sends.append(remote(src, kv_land.at[:, side, y], to, kv_send.at[i], kv_recv))
        sends[-1].start()
    local(kv_here.at[:, :, cols(head * 128, 128)], kv_land.at[:, side, y], kv_recv).start()
    for half in range(2):
        src = q_here.at[:, cols(head * 1024 + half * HALF, HALF)]
        local(src, q_land.at[half, side, y], q_recv.at[half]).start()
        for i in (6, 5, 7, 2, 4, 1, 3):
            to, their_side, their_y = partner(i)
            src = q_here.at[:, cols((their_y * 2 + their_side) * 1024 + half * HALF, HALF)]
            sends.append(
                remote(src, q_land.at[half, side, y], to, q_send.at[half, i], q_recv.at[half])
            )
            sends[-1].start()
    sends.append(remote(codes.at[0], codes.at[1], partner(4)[0], t_send, t_recv))
    sends[-1].start()

    def z_copy(role, way, step):
        src, dst = ((8 - step) % 8, 7 - step) if way == 0 else (step, step + 1)
        pick = (role,) if step < 3 else (role, pl.ds(way * 128, 128))
        return remote(
            kv.at[(src, c) + pick], kv.at[(dst, c) + pick], z_ways[way],
            z_send.at[role, way, step], z_recv.at[role, way, step],
        )

    def first_cross():
        return remote(kv.at[0, c, 1], kv.at[0, c, 2], across, x_send.at[8], x_recv.at[8])

    def cross(dz):
        return remote(
            kv.at[dz, c, 0], kv.at[dz, c, 2 + pair], across, x_send.at[dz], x_recv.at[dz]
        )

    def to_sibling(role, dz):
        ref = kv.at[dz, c, role]
        return remote(ref, ref, sibling, s_send.at[role, dz], s_recv.at[role, dz])

    def on_pair(which):
        return pl.when(pair == which)

    def take(role, d):
        if d < 4:
            for way, dz in ((0, 8 - d), (1, d)):
                z_copy(role, way, d - 1).wait_recv()
                z_copy(role, way, d).start()
                if role == 0:
                    cross(dz).start()
                to_sibling(role, dz).start()
        else:
            z_copy(role, 0, 3).wait_recv()
            z_copy(role, 1, 3).wait_recv()
            if role == 0:
                cross(4).start()
            to_sibling(role, 4).start()

    def crossed(dzs):
        for dz in dzs:
            cross(dz).wait_recv()
            to_sibling(3 - pair, dz).start()

    def heard(roles, dzs):
        for role in roles:
            for dz in dzs:
                to_sibling(role, dz).wait_recv()

    arrived(kv_land, kv_recv)
    for which in range(2):
        kv[0, c, which, 0:128, :] = kv_land[0, which].reshape(128, HEAD_DIM)
        kv[0, c, which, 128:256, :] = kv_land[1, which].reshape(128, HEAD_DIM).T

    @on_pair(1)
    def _():
        first_cross().start()

    for role in range(2):
        z_copy(role, 0, 0).start()
        z_copy(role, 1, 0).start()
        to_sibling(role, 0).start()
        if role == 0:
            cross(0).start()

    @on_pair(0)
    def _():
        first_cross().wait_recv()
        z_copy(2, 0, 0).start()
        z_copy(2, 1, 0).start()
        to_sibling(2, 0).start()

    crossed((0,))

    def queries_of(which, heads):
        parts = []
        for h in heads:
            q = q_land[h // 4, which, :, :, h % 4 * 128 : (h % 4 + 1) * 128]
            parts.append(q.reshape(128, HEAD_DIM))
        return jnp.concatenate(parts, axis=0)

    def attend(which, heads, blocks):
        q = queries_of(which, heads)
        spot = slice(heads[0] * 128, heads[-1] * 128 + 128)
        scores = []
        for role, dzs, kind in blocks:
            key = jnp.concatenate(
                [kv[dz, core, role, 0:128, :] for dz in dzs for core in range(2)], axis=0
            )
            part = lax.dot_general(key, q, NT, preferred_element_type=jnp.float32)
            if kind == "diagonal":
                row = lax.broadcasted_iota(jnp.int32, (256, 1), 0)
                key_pos = (row % 128 // 32) * 64 + (row // 128) * 32 + row % 32
                token = lax.broadcasted_iota(jnp.int32, (1, q.shape[0]), 1) % 128
                query_pos = (token // 32) * 64 + c * 32 + token % 32
                part = jnp.where(key_pos <= query_pos, part, LOW)
            scores.append(part)
        old, total = top[which, :, spot], acc[which, :, spot]
        for (role, dzs, kind), part in zip(blocks, scores):
            if kind == "earlier":
                new, weights = old, []
                for n, dz in enumerate(dzs):
                    high = jnp.max(part[n * 256 : (n + 1) * 256], axis=0, keepdims=True)
                    new = jnp.where(z + dz >= 8, jnp.maximum(new, high), new)
                for n, dz in enumerate(dzs):
                    base = jnp.where(z + dz >= 8, new[0:1], -LOW)
                    weights.append(
                        jnp.exp2((part[n * 256 : (n + 1) * 256] - base) * SCALE).astype(jnp.bfloat16)
                    )
                weights = jnp.concatenate(weights, axis=0)
            else:
                new = jnp.maximum(old, jnp.max(part, axis=0, keepdims=True))
                weights = jnp.exp2((part - new[0:1]) * SCALE).astype(jnp.bfloat16)
            value = jnp.concatenate(
                [kv[dz, core, role, 128:256, :] for dz in dzs for core in range(2)], axis=1
            )
            value = jnp.concatenate([value, jnp.ones((16, value.shape[1]), jnp.bfloat16)], axis=0)
            product = jnp.dot(value, weights, preferred_element_type=jnp.float32)
            total = total * jnp.exp2((old - new) * SCALE)[0:1] + product
            old = new
        top[which, :, spot] = old
        acc[which, :, spot] = total

    def own_units(heads, dzs, kind):
        if kind == "diagonal":
            attend(1, heads, [(0, dzs, "all"), (1, dzs, kind)])
            attend(0, heads, [(0, dzs, kind)])
            return
        some = z + max(dzs) >= 8

        @pl.when(some)
        def _():
            attend(1, heads, [(0, dzs, "all"), (1, dzs, kind)])
            attend(0, heads, [(0, dzs, kind)])

        @pl.when(jnp.logical_not(some))
        def _():
            attend(1, heads, [(0, dzs, "all")])

    def other_units(heads, dzs):
        @on_pair(0)
        def _():
            attend(1, heads, [(2, dzs, "all"), (3, dzs, "all")])

        @on_pair(1)
        def _():
            attend(1, heads, [(2, dzs, "all")])
            attend(0, heads, [(2, dzs, "all")])

    everything = range(8)
    halves = (range(4), range(4, 8))

    def place_pages():
        for which in range(2):
            code = jnp.where(side == which, codes[0], codes[1])
            spot = lax.broadcasted_iota(jnp.int32, (128, 1024), 1)
            entry = lax.broadcasted_iota(jnp.int32, (128, 1024), 0)
            page = (spot // 256) * 16 + (spot % 128 // 32) * 4 + (spot % 256 // 128) * 2 + spot % 32 // 16
            spread = jnp.where(entry == page, 1.0, 0.0).astype(jnp.bfloat16)
            token = jnp.dot(code.astype(jnp.bfloat16), spread, preferred_element_type=jnp.float32)
            token = token[0:1].astype(jnp.int32) * 16 + spot[0:1] % 16
            row = lax.broadcasted_iota(jnp.int32, (256, 1), 0)
            target = (z_lo * 8 + (row // 64) * 2 + c) * 4 + row // 16 % 4
            pick = jnp.where(target * 16 + row % 16 == token, 1.0, 0.0).astype(jnp.bfloat16)
            parts = [(lax.rem(lo + 8 - z_lo, 8), core) for lo in range(4) for core in range(2)]
            key = jnp.concatenate([kv[dz, core, which, 0:128, :] for dz, core in parts], axis=0)
            value = jnp.concatenate([kv[dz, core, which, 128:256, :] for dz, core in parts], axis=1)
            found = jnp.dot(pick, key, preferred_element_type=jnp.float32)
            pages[0, which] = found.astype(jnp.bfloat16).reshape(16, 16, HEAD_DIM)
            found = lax.dot_general(pick, value, NT, preferred_element_type=jnp.float32)
            pages[1, which] = found.astype(jnp.bfloat16).reshape(16, 16, HEAD_DIM)

    def page_copy(i, which):
        to, their_side, their_y = partner(i)
        cache = (key_cache, value_cache)[which]
        src = pages.at[which, their_side, pl.ds(their_y * 4, 4)]
        dst = cache.at[:, :, cols(head * 128, 128)]
        if i == 0:
            return local(src, dst, g_recv.at[which])
        return remote(src, dst, to, g_send.at[which, i], g_recv.at[which])

    def o_copy(which, half, j):
        src = o_stage.at[which, half, ys[j]]
        dst = att.at[:, cols(head * 1024 + half * HALF, HALF)]
        xx = jnp.where(side == which, x, 3 - x)
        to = (xx * 2 + z_hi, z_lo * 8 + ys[j] * 2 + c)
        return src, dst, to, o_send.at[which, half, ys[j]]

    def finish(which, half):
        done = acc[which, 0:128, half * 512 : (half + 1) * 512]
        done = done / acc[which, 128:129, half * 512 : (half + 1) * 512]
        for h in range(4):
            o_stage[which, half, :, :, h * 128 : (h + 1) * 128] = (
                done[:, h * 128 : (h + 1) * 128].T.astype(jnp.bfloat16).reshape(4, ROWS, HEAD_DIM)
            )

    def send_finished(which, half):
        for j in (2, 1, 3):
            src, dst, to, sem = o_copy(which, half, j)
            remote(src, dst, to, sem, o_recv).start()
        src, dst, to, sem = o_copy(which, half, 0)

        @pl.when(side == which)
        def _():
            local(src, dst, o_recv).start()

        @pl.when(side != which)
        def _():
            remote(src, dst, to, sem, o_recv).start()

    heard((0, 1), (0,))
    arrived(q_land.at[0], q_recv.at[0])
    own_units(halves[0], (0,), "diagonal")
    take(0, 1)
    take(1, 1)
    heard((2,), (0,))

    @on_pair(0)
    def _():
        heard((3,), (0,))

    other_units(halves[0], (0,))

    @on_pair(0)
    def _():
        take(2, 1)

    arrived(q_land.at[1], q_recv.at[1])
    own_units(halves[1], (0,), "diagonal")
    other_units(halves[1], (0,))

    for d in range(1, 4):
        both = (8 - d, d)
        take(0, d + 1)
        crossed(both)
        heard((0, 1), both)
        own_units(everything, both, "earlier")
        take(1, d + 1)

        @on_pair(0)
        def _():
            take(2, d + 1)

        if d == 3:
            arrived(codes.at[1], t_recv)
            place_pages()
            for which in range(2):
                for i in range(GROUP):
                    page_copy(i, which).start()
        heard((2,), both)

        @on_pair(0)
        def _():
            heard((3,), both)

        other_units(everything, both)

    crossed((4,))
    heard((0, 1), (4,))
    for half in range(2):
        own_units(halves[half], (4,), "earlier")

    @on_pair(0)
    def _():
        for half in range(2):
            finish(0, half)
            send_finished(0, half)

    heard((2,), (4,))

    @on_pair(0)
    def _():
        heard((3,), (4,))
        for half in range(2):
            attend(1, halves[half], [(2, (4,), "all"), (3, (4,), "all")])
            finish(1, half)
            send_finished(1, half)

    @on_pair(1)
    def _():
        for which in (1, 0):
            for half in range(2):
                attend(which, halves[half], [(2, (4,), "all")])
                finish(which, half)
                send_finished(which, half)

    for copy in sends:
        copy.wait_send()
    for role in range(2):
        for way in range(2):
            for step in range(4):
                z_copy(role, way, step).wait_send()
    for dz in range(8):
        cross(dz).wait_send()
        for role in range(3):
            to_sibling(role, dz).wait_send()

    @on_pair(0)
    def _():
        for way in range(2):
            for step in range(4):
                z_copy(2, way, step).wait_send()
        for dz in range(8):
            to_sibling(3, dz).wait_send()

    @on_pair(1)
    def _():
        first_cross().wait_send()

    for which in range(2):
        for i in range(1, GROUP):
            page_copy(i, which).wait_send()
    for which in range(2):
        for half in range(2):
            for j in range(1, 4):
                src, dst, to, sem = o_copy(which, half, j)
                remote(src, dst, to, sem, o_recv).wait_send()

        @pl.when(side != which)
        def _():
            for half in range(2):
                src, dst, to, sem = o_copy(which, half, 0)
                remote(src, dst, to, sem, o_recv).wait_send()

    arrived(key_cache, g_recv.at[0])
    arrived(value_cache, g_recv.at[1])
    arrived(att, o_recv)


def move(att, key_cache, value_cache, att_out, key_out, value_out, held, held_key, held_value, sem):
    parts = [(key_cache, held_key, key_out), (value_cache, held_value, value_out)]
    for n in range(4):
        columns = pl.ds(n * 2048, 2048)
        parts.append((att.at[:, columns], held.at[:, columns], att_out.at[:, columns]))
    loads = [pltpu.make_async_copy(src, at, sem.at[0, n]) for n, (src, at, _) in enumerate(parts)]
    stores = [pltpu.make_async_copy(at, dst, sem.at[1, n]) for n, (_, at, dst) in enumerate(parts)]
    for load in loads:
        load.start()
    for load, store in zip(loads, stores):
        load.wait()
        store.start()
    for store in stores:
        store.wait()


def shards(queries, key_rows, value_rows, page_owner, page_slot):
    dma = pltpu.SemaphoreType.DMA
    bf16 = jnp.bfloat16
    anywhere = pl.BlockSpec(memory_space=pl.ANY)
    held = pl.pallas_call(
        kernel,
        out_shape=(
            jax.ShapeDtypeStruct(queries.shape, bf16),
            jax.ShapeDtypeStruct((4, 16, 1024), bf16),
            jax.ShapeDtypeStruct((4, 16, 1024), bf16),
        ),
        in_specs=[anywhere] * 3 + [pl.BlockSpec(memory_space=pltpu.SMEM)] * 2,
        out_specs=(anywhere,) * 3,
        scratch_shapes=[
            pltpu.VMEM((ROWS, 8192), bf16),
            pltpu.VMEM((2, ROWS, 1024), bf16),
            pltpu.VMEM((2, 2, 4, ROWS, HALF), bf16),
            pltpu.VMEM((2, 2, 4, ROWS, HEAD_DIM), bf16),
            pltpu.VMEM((8, 2, 4, 256, HEAD_DIM), bf16),
            pltpu.VMEM((2, 144, SET), jnp.float32),
            pltpu.VMEM((2, 8, SET), jnp.float32),
            pltpu.VMEM((2, 2, 4, ROWS, HALF), bf16),
            pltpu.VMEM((2, 2, 16, 16, HEAD_DIM), bf16),
            pltpu.VMEM((2, 8, 128), jnp.int32),
            dma((3,)),
            dma((GROUP,)),
            dma,
            dma,
            dma,
            dma((2, GROUP)),
            dma((2,)),
            dma((3, 2, 4)),
            dma((3, 2, 4)),
            dma((9,)),
            dma((9,)),
            dma((4, 8)),
            dma((4, 8)),
            dma((2, 2, 4)),
            dma,
            dma((2, GROUP)),
            dma((2,)),
        ],
        compiler_params=pltpu.CompilerParams(
            collective_id=0, has_side_effects=True, vmem_limit_bytes=56 * 2**20
        ),
    )(queries, key_rows, value_rows, page_owner, page_slot)
    return pl.pallas_call(
        move,
        out_shape=tuple(jax.ShapeDtypeStruct(a.shape, bf16) for a in held),
        in_specs=[anywhere] * 3,
        out_specs=(anywhere,) * 3,
        scratch_shapes=[pltpu.VMEM(a.shape, bf16) for a in held] + [dma((2, 6))],
    )(*held)


def solution(mesh):
    whole = P(("ctx", "serve"), None)
    return jax.shard_map(
        shards,
        mesh=mesh,
        in_specs=(whole, whole, whole, P("ctx"), P("ctx")),
        out_specs=(whole, P(("ctx", "serve"), None, None), P(("ctx", "serve"), None, None)),
        check_vma=False,
    )
```

```python
import math

import jax
import jax.numpy as jnp
from jax import lax
from jax.experimental import pallas as pl
from jax.experimental.pallas import tpu as pltpu
from jax.sharding import PartitionSpec as P

HEAD_DIM = 128
ROWS = 32
GROUP = 8
SET = 1024
HALF = 512
SCALE = math.log2(math.e) / math.sqrt(HEAD_DIM)
LOW = -1e30
NT = (((1,), (1,)), ((), ()))
MESH = pl.DeviceIdType.MESH


def kernel(
    q_in, k_in, v_in, owner, slot,
    att, key_cache, value_cache,
    q_here, kv_here, q_land, kv_land, kv, acc, top, o_stage, pages, codes,
    in_sem, kv_send, kv_recv, t_send, t_recv, q_send, q_recv, z_send, z_recv, x_send, x_recv,
    s_send, s_recv, o_send, o_recv, g_send, g_recv,
):
    ctx = lax.axis_index("ctx")
    serve = lax.axis_index("serve")
    x, z_hi = lax.div(ctx, 2), lax.rem(ctx, 2)
    z_lo, low = lax.div(serve, 8), lax.rem(serve, 8)
    y, c = lax.div(low, 2), lax.rem(low, 2)
    z = z_hi * 4 + z_lo
    side, x_odd = lax.div(x, 2), lax.rem(x, 2)
    pair = side + x_odd - 2 * side * x_odd
    x_other = x + 1 - 2 * x_odd
    xs, sides = (x, 3 - x), (side, 1 - side)
    y_odd, y_big = lax.rem(y, 2), lax.div(y, 2)
    ys = (y, y + 1 - 2 * y_odd, y + 2 - 4 * y_big, 3 - y)
    head = y * 2 + side

    def device(xx, zz, yy, cc):
        hi = lax.div(zz, 4)
        return (xx * 2 + hi, (zz - hi * 4) * 8 + yy * 2 + cc)

    def partner(i):
        xx, yy = xs[i // 4], ys[i % 4]
        return (xx * 2 + z_hi, z_lo * 8 + yy * 2 + c), sides[i // 4], yy

    sibling = (ctx, serve + 1 - 2 * c)
    z_ways = (device(x, lax.rem(z + 1, 8), y, c), device(x, lax.rem(z + 7, 8), y, c))
    across = (x_other * 2 + z_hi, serve)

    loads = [
        pltpu.make_async_copy(k_in, kv_here.at[0], in_sem.at[0]),
        pltpu.make_async_copy(v_in, kv_here.at[1], in_sem.at[1]),
        pltpu.make_async_copy(q_in, q_here, in_sem.at[2]),
    ]
    barrier = pltpu.get_barrier_semaphore()
    peers = [z_ways[0], z_ways[1], across, sibling] + [partner(i)[0] for i in range(1, GROUP)]
    for peer in peers:
        pl.semaphore_signal(barrier, inc=1, device_id=peer, device_id_type=MESH)
    for load in loads:
        load.start()
    acc[...] = jnp.zeros_like(acc)
    top[...] = jnp.full_like(top, LOW)
    lane = lax.broadcasted_iota(jnp.int32, (8, 128), 1)
    table = jnp.zeros((8, 128), jnp.int32)
    for i in range(64):
        table = jnp.where(lane == i, owner[i] * 4 + slot[i], table)
    codes[0] = table
    for load in loads:
        load.wait()
    pl.semaphore_wait(barrier, len(peers))

    def cols(start, size):
        return pl.ds(pl.multiple_of(start, 128), size)

    def remote(src, dst, to, send, recv):
        return pltpu.make_async_remote_copy(
            src_ref=src, dst_ref=dst, send_sem=send, recv_sem=recv,
            device_id=to, device_id_type=MESH,
        )

    def local(src, dst, sem):
        return pltpu.make_async_copy(src, dst, sem)

    def arrived(ref, sem):
        pltpu.make_async_copy(ref, ref, sem).wait()

    sends = []
    for i in (6, 5, 7, 2, 4, 1, 3):
        to, their_side, their_y = partner(i)
        src = kv_here.at[:, :, cols((their_y * 2 + their_side) * 128, 128)]
        sends.append(remote(src, kv_land.at[:, side, y], to, kv_send.at[i], kv_recv))
        sends[-1].start()
    local(kv_here.at[:, :, cols(head * 128, 128)], kv_land.at[:, side, y], kv_recv).start()
    for half in range(2):
        src = q_here.at[:, cols(head * 1024 + half * HALF, HALF)]
        local(src, q_land.at[half, side, y], q_recv.at[half]).start()
        for i in (6, 5, 7, 2, 4, 1, 3):
            to, their_side, their_y = partner(i)
            src = q_here.at[:, cols((their_y * 2 + their_side) * 1024 + half * HALF, HALF)]
            sends.append(
                remote(src, q_land.at[half, side, y], to, q_send.at[half, i], q_recv.at[half])
            )
            sends[-1].start()
    sends.append(remote(codes.at[0], codes.at[1], partner(4)[0], t_send, t_recv))
    sends[-1].start()

    def z_copy(role, way, step):
        src, dst = ((8 - step) % 8, 7 - step) if way == 0 else (step, step + 1)
        pick = (role,) if step < 3 else (role, pl.ds(way * 128, 128))
        return remote(
            kv.at[(src, c) + pick], kv.at[(dst, c) + pick], z_ways[way],
            z_send.at[role, way, step], z_recv.at[role, way, step],
        )

    def first_cross():
        return remote(kv.at[0, c, 1], kv.at[0, c, 2], across, x_send.at[8], x_recv.at[8])

    def cross(dz):
        return remote(
            kv.at[dz, c, 0], kv.at[dz, c, 2 + pair], across, x_send.at[dz], x_recv.at[dz]
        )

    def to_sibling(role, dz):
        ref = kv.at[dz, c, role]
        return remote(ref, ref, sibling, s_send.at[role, dz], s_recv.at[role, dz])

    def on_pair(which):
        return pl.when(pair == which)

    def take(role, d):
        if d < 4:
            for way, dz in ((0, 8 - d), (1, d)):
                z_copy(role, way, d - 1).wait_recv()
                z_copy(role, way, d).start()
                if role == 0:
                    cross(dz).start()
                to_sibling(role, dz).start()
        else:
            z_copy(role, 0, 3).wait_recv()
            z_copy(role, 1, 3).wait_recv()
            if role == 0:
                cross(4).start()
            to_sibling(role, 4).start()

    def crossed(dzs):
        for dz in dzs:
            cross(dz).wait_recv()
            to_sibling(3 - pair, dz).start()

    def heard(roles, dzs):
        for role in roles:
            for dz in dzs:
                to_sibling(role, dz).wait_recv()

    arrived(kv_land, kv_recv)
    for which in range(2):
        kv[0, c, which, 0:128, :] = kv_land[0, which].reshape(128, HEAD_DIM)
        kv[0, c, which, 128:256, :] = kv_land[1, which].reshape(128, HEAD_DIM).T

    @on_pair(1)
    def _():
        first_cross().start()

    for role in range(2):
        z_copy(role, 0, 0).start()
        z_copy(role, 1, 0).start()
        to_sibling(role, 0).start()
        if role == 0:
            cross(0).start()

    @on_pair(0)
    def _():
        first_cross().wait_recv()
        z_copy(2, 0, 0).start()
        z_copy(2, 1, 0).start()
        to_sibling(2, 0).start()

    crossed((0,))

    def queries_of(which, heads):
        parts = []
        for h in heads:
            q = q_land[h // 4, which, :, :, h % 4 * 128 : (h % 4 + 1) * 128]
            parts.append(q.reshape(128, HEAD_DIM))
        return jnp.concatenate(parts, axis=0)

    def attend(which, heads, blocks):
        q = queries_of(which, heads)
        spot = slice(heads[0] * 128, heads[-1] * 128 + 128)
        scores = []
        for role, dzs, kind in blocks:
            key = jnp.concatenate(
                [kv[dz, core, role, 0:128, :] for dz in dzs for core in range(2)], axis=0
            )
            part = lax.dot_general(key, q, NT, preferred_element_type=jnp.float32)
            if kind == "diagonal":
                row = lax.broadcasted_iota(jnp.int32, (256, 1), 0)
                key_pos = (row % 128 // 32) * 64 + (row // 128) * 32 + row % 32
                token = lax.broadcasted_iota(jnp.int32, (1, q.shape[0]), 1) % 128
                query_pos = (token // 32) * 64 + c * 32 + token % 32
                part = jnp.where(key_pos <= query_pos, part, LOW)
            scores.append(part)
        old, total = top[which, :, spot], acc[which, :, spot]
        for (role, dzs, kind), part in zip(blocks, scores):
            if kind == "earlier":
                new, weights = old, []
                for n, dz in enumerate(dzs):
                    high = jnp.max(part[n * 256 : (n + 1) * 256], axis=0, keepdims=True)
                    new = jnp.where(z + dz >= 8, jnp.maximum(new, high), new)
                for n, dz in enumerate(dzs):
                    base = jnp.where(z + dz >= 8, new[0:1], -LOW)
                    weights.append(
                        jnp.exp2((part[n * 256 : (n + 1) * 256] - base) * SCALE).astype(jnp.bfloat16)
                    )
                weights = jnp.concatenate(weights, axis=0)
            else:
                new = jnp.maximum(old, jnp.max(part, axis=0, keepdims=True))
                weights = jnp.exp2((part - new[0:1]) * SCALE).astype(jnp.bfloat16)
            value = jnp.concatenate(
                [kv[dz, core, role, 128:256, :] for dz in dzs for core in range(2)], axis=1
            )
            value = jnp.concatenate([value, jnp.ones((16, value.shape[1]), jnp.bfloat16)], axis=0)
            product = jnp.dot(value, weights, preferred_element_type=jnp.float32)
            total = total * jnp.exp2((old - new) * SCALE)[0:1] + product
            old = new
        top[which, :, spot] = old
        acc[which, :, spot] = total

    def own_units(heads, dzs, kind):
        if kind == "diagonal":
            attend(1, heads, [(0, dzs, "all"), (1, dzs, kind)])
            attend(0, heads, [(0, dzs, kind)])
            return
        every, some = z + min(dzs) >= 8, z + max(dzs) >= 8

        @pl.when(every)
        def _():
            attend(1, heads, [(0, dzs, "all"), (1, dzs, "all")])
            attend(0, heads, [(0, dzs, "all")])

        if len(dzs) > 1:

            @pl.when(some & jnp.logical_not(every))
            def _():
                attend(1, heads, [(0, dzs, "all"), (1, (max(dzs),), "all")])
                attend(0, heads, [(0, (max(dzs),), "all")])

        @pl.when(jnp.logical_not(some))
        def _():
            attend(1, heads, [(0, dzs, "all")])

    def other_units(heads, dzs):
        @on_pair(0)
        def _():
            attend(1, heads, [(2, dzs, "all"), (3, dzs, "all")])

        @on_pair(1)
        def _():
            attend(1, heads, [(2, dzs, "all")])
            attend(0, heads, [(2, dzs, "all")])

    everything = range(8)
    halves = (range(4), range(4, 8))

    def place_pages():
        for which in range(2):
            code = jnp.where(side == which, codes[0], codes[1])
            spot = lax.broadcasted_iota(jnp.int32, (128, 1024), 1)
            entry = lax.broadcasted_iota(jnp.int32, (128, 1024), 0)
            page = (spot // 256) * 16 + (spot % 128 // 32) * 4 + (spot % 256 // 128) * 2 + spot % 32 // 16
            spread = jnp.where(entry == page, 1.0, 0.0).astype(jnp.bfloat16)
            token = jnp.dot(code.astype(jnp.bfloat16), spread, preferred_element_type=jnp.float32)
            token = token[0:1].astype(jnp.int32) * 16 + spot[0:1] % 16
            row = lax.broadcasted_iota(jnp.int32, (256, 1), 0)
            target = (z_lo * 8 + (row // 64) * 2 + c) * 4 + row // 16 % 4
            pick = jnp.where(target * 16 + row % 16 == token, 1.0, 0.0).astype(jnp.bfloat16)
            parts = [(lax.rem(lo + 8 - z_lo, 8), core) for lo in range(4) for core in range(2)]
            key = jnp.concatenate([kv[dz, core, which, 0:128, :] for dz, core in parts], axis=0)
            value = jnp.concatenate([kv[dz, core, which, 128:256, :] for dz, core in parts], axis=1)
            found = jnp.dot(pick, key, preferred_element_type=jnp.float32)
            pages[0, which] = found.astype(jnp.bfloat16).reshape(16, 16, HEAD_DIM)
            found = lax.dot_general(pick, value, NT, preferred_element_type=jnp.float32)
            pages[1, which] = found.astype(jnp.bfloat16).reshape(16, 16, HEAD_DIM)

    def page_copy(i, which):
        to, their_side, their_y = partner(i)
        cache = (key_cache, value_cache)[which]
        src = pages.at[which, their_side, pl.ds(their_y * 4, 4)]
        dst = cache.at[:, :, cols(head * 128, 128)]
        if i == 0:
            return local(src, dst, g_recv.at[which])
        return remote(src, dst, to, g_send.at[which, i], g_recv.at[which])

    def o_copy(which, half, j):
        src = o_stage.at[which, half, ys[j]]
        dst = att.at[:, cols(head * 1024 + half * HALF, HALF)]
        xx = jnp.where(side == which, x, 3 - x)
        to = (xx * 2 + z_hi, z_lo * 8 + ys[j] * 2 + c)
        return src, dst, to, o_send.at[which, half, ys[j]]

    def finish(which, half):
        done = acc[which, 0:128, half * 512 : (half + 1) * 512]
        done = done / acc[which, 128:129, half * 512 : (half + 1) * 512]
        for h in range(4):
            o_stage[which, half, :, :, h * 128 : (h + 1) * 128] = (
                done[:, h * 128 : (h + 1) * 128].T.astype(jnp.bfloat16).reshape(4, ROWS, HEAD_DIM)
            )

    def send_finished(which, half):
        for j in (2, 1, 3):
            src, dst, to, sem = o_copy(which, half, j)
            remote(src, dst, to, sem, o_recv).start()
        src, dst, to, sem = o_copy(which, half, 0)

        @pl.when(side == which)
        def _():
            local(src, dst, o_recv).start()

        @pl.when(side != which)
        def _():
            remote(src, dst, to, sem, o_recv).start()

    heard((0, 1), (0,))
    arrived(q_land.at[0], q_recv.at[0])
    own_units(halves[0], (0,), "diagonal")
    take(0, 1)
    take(1, 1)
    heard((2,), (0,))

    @on_pair(0)
    def _():
        heard((3,), (0,))

    other_units(halves[0], (0,))

    @on_pair(0)
    def _():
        take(2, 1)

    arrived(q_land.at[1], q_recv.at[1])
    own_units(halves[1], (0,), "diagonal")
    other_units(halves[1], (0,))

    for d in range(1, 4):
        both = (8 - d, d)
        take(0, d + 1)
        crossed(both)
        heard((0, 1), both)
        own_units(everything, both, "earlier")
        take(1, d + 1)

        @on_pair(0)
        def _():
            take(2, d + 1)

        if d == 3:
            arrived(codes.at[1], t_recv)
            place_pages()
            for which in range(2):
                for i in range(GROUP):
                    page_copy(i, which).start()
        heard((2,), both)

        @on_pair(0)
        def _():
            heard((3,), both)

        other_units(everything, both)

    crossed((4,))
    heard((0, 1), (4,))
    for half in range(2):
        own_units(halves[half], (4,), "earlier")

    @on_pair(0)
    def _():
        for half in range(2):
            finish(0, half)
            send_finished(0, half)

    heard((2,), (4,))

    @on_pair(0)
    def _():
        heard((3,), (4,))
        for half in range(2):
            attend(1, halves[half], [(2, (4,), "all"), (3, (4,), "all")])
            finish(1, half)
            send_finished(1, half)

    @on_pair(1)
    def _():
        for which in (1, 0):
            for half in range(2):
                attend(which, halves[half], [(2, (4,), "all")])
                finish(which, half)
                send_finished(which, half)

    for copy in sends:
        copy.wait_send()
    for role in range(2):
        for way in range(2):
            for step in range(4):
                z_copy(role, way, step).wait_send()
    for dz in range(8):
        cross(dz).wait_send()
        for role in range(3):
            to_sibling(role, dz).wait_send()

    @on_pair(0)
    def _():
        for way in range(2):
            for step in range(4):
                z_copy(2, way, step).wait_send()
        for dz in range(8):
            to_sibling(3, dz).wait_send()

    @on_pair(1)
    def _():
        first_cross().wait_send()

    for which in range(2):
        for i in range(1, GROUP):
            page_copy(i, which).wait_send()
    for which in range(2):
        for half in range(2):
            for j in range(1, 4):
                src, dst, to, sem = o_copy(which, half, j)
                remote(src, dst, to, sem, o_recv).wait_send()

        @pl.when(side != which)
        def _():
            for half in range(2):
                src, dst, to, sem = o_copy(which, half, 0)
                remote(src, dst, to, sem, o_recv).wait_send()

    arrived(key_cache, g_recv.at[0])
    arrived(value_cache, g_recv.at[1])
    arrived(att, o_recv)


def move(att, key_cache, value_cache, att_out, key_out, value_out, held, held_key, held_value, sem):
    parts = [(key_cache, held_key, key_out), (value_cache, held_value, value_out)]
    for n in range(4):
        columns = pl.ds(n * 2048, 2048)
        parts.append((att.at[:, columns], held.at[:, columns], att_out.at[:, columns]))
    loads = [pltpu.make_async_copy(src, at, sem.at[0, n]) for n, (src, at, _) in enumerate(parts)]
    stores = [pltpu.make_async_copy(at, dst, sem.at[1, n]) for n, (_, at, dst) in enumerate(parts)]
    for load in loads:
        load.start()
    for load, store in zip(loads, stores):
        load.wait()
        store.start()
    for store in stores:
        store.wait()


def shards(queries, key_rows, value_rows, page_owner, page_slot):
    dma = pltpu.SemaphoreType.DMA
    bf16 = jnp.bfloat16
    anywhere = pl.BlockSpec(memory_space=pl.ANY)
    held = pl.pallas_call(
        kernel,
        out_shape=(
            jax.ShapeDtypeStruct(queries.shape, bf16),
            jax.ShapeDtypeStruct((4, 16, 1024), bf16),
            jax.ShapeDtypeStruct((4, 16, 1024), bf16),
        ),
        in_specs=[anywhere] * 3 + [pl.BlockSpec(memory_space=pltpu.SMEM)] * 2,
        out_specs=(anywhere,) * 3,
        scratch_shapes=[
            pltpu.VMEM((ROWS, 8192), bf16),
            pltpu.VMEM((2, ROWS, 1024), bf16),
            pltpu.VMEM((2, 2, 4, ROWS, HALF), bf16),
            pltpu.VMEM((2, 2, 4, ROWS, HEAD_DIM), bf16),
            pltpu.VMEM((8, 2, 4, 256, HEAD_DIM), bf16),
            pltpu.VMEM((2, 144, SET), jnp.float32),
            pltpu.VMEM((2, 8, SET), jnp.float32),
            pltpu.VMEM((2, 2, 4, ROWS, HALF), bf16),
            pltpu.VMEM((2, 2, 16, 16, HEAD_DIM), bf16),
            pltpu.VMEM((2, 8, 128), jnp.int32),
            dma((3,)),
            dma((GROUP,)),
            dma,
            dma,
            dma,
            dma((2, GROUP)),
            dma((2,)),
            dma((3, 2, 4)),
            dma((3, 2, 4)),
            dma((9,)),
            dma((9,)),
            dma((4, 8)),
            dma((4, 8)),
            dma((2, 2, 4)),
            dma,
            dma((2, GROUP)),
            dma((2,)),
        ],
        compiler_params=pltpu.CompilerParams(
            collective_id=0, has_side_effects=True, vmem_limit_bytes=56 * 2**20
        ),
    )(queries, key_rows, value_rows, page_owner, page_slot)
    return pl.pallas_call(
        move,
        out_shape=tuple(jax.ShapeDtypeStruct(a.shape, bf16) for a in held),
        in_specs=[anywhere] * 3,
        out_specs=(anywhere,) * 3,
        scratch_shapes=[pltpu.VMEM(a.shape, bf16) for a in held] + [dma((2, 6))],
    )(*held)


def solution(mesh):
    whole = P(("ctx", "serve"), None)
    return jax.shard_map(
        shards,
        mesh=mesh,
        in_specs=(whole, whole, whole, P("ctx"), P("ctx")),
        out_specs=(whole, P(("ctx", "serve"), None, None), P(("ctx", "serve"), None, None)),
        check_vma=False,
    )
```
